256 devices in a mesh: expert: 32 (over z, x), replica: 4 (over y), section: 2 (over core).
Axes of the slice: x: 4, y: 4, z: 8, core: 2. Of those that a mesh axis runs over, the one named last changes fastest.
Arguments:
- frames: bfloat16 [2, 16384, 1024], P('section', ('expert', 'replica')), may hold values from -6 to 6
- cotangent: bfloat16 [2, 16384, 1024], P('section', ('expert', 'replica')), may hold values from -3 to 3
- expert_ids: int32 [2, 16384, 8], P('section', ('expert', 'replica')), may hold values from 0 to 63, all different within a row; in each aligned block of 128 rows (0 to 127, 128 to 255, ..., all dimensions but the last counted through in order) at most 24 rows name the same one
- gate_weights: float32 [2, 16384, 8], P('section', ('expert', 'replica')), may hold values from 0.05 to 1
- weight_in: bfloat16 [2, 64, 1024, 768], P('section', 'expert', 'replica'), may hold values from -0.1875 to 0.1875
- weight_out: bfloat16 [2, 64, 768, 1024], P('section', 'expert', None, 'replica'), may hold values from -0.21875 to 0.21875
Outputs:
- sent_grads: bfloat16 [2, 16384, 1024], P('section', ('expert', 'replica'))
- grad_in: bfloat16 [2, 64, 1024, 768], P('section', 'expert', 'replica')
- grad_out: bfloat16 [2, 64, 768, 1024], P('section', 'expert', None, 'replica')
The draws below stay inside these ranges and needn't reach their ends.
Inputs may be any that keep to these rules, and one draw needn't show every extreme that they name: `expert_ids`: each row names 8 different experts; among the rows of one device no expert is named more than 24 times, a bound that some block reaches.
All inputs are finite; a program needn't handle non-finite values.
Results may differ from the reference program's by a relative error of at most 0.012.
Values may be sent and summed in bfloat16 or wider, within the bound.
A program may use at most 64 MiB of HBM per device.

```python
import math
import jax
import jax.numpy as jnp
import numpy as np
from jax import lax

D = 1024
H = 768
TOPK = 8
TOK_DEV = 128
EXPERTS = 64
MOST = 24
TOKENS = 16384
N_EXPERT = 32
N_REPLICA = 4


def shard_levels(own_key, extent, split, smallest, high):
    factor_of, own = 1.0, jax.random.fold_in(own_key, 6)
    for axis_at, parts in split:
        steps = jnp.exp(jax.random.uniform(jax.random.fold_in(own, axis_at), (parts,), jnp.float32, smallest / len(split), high / len(split)))
        factor_of = factor_of * jnp.repeat(steps, extent[axis_at] // parts).reshape([-1 if axis == axis_at else 1 for axis in range(len(extent))])
    return factor_of


def assign_block(own_key, own, number, rows, amount, top, limit, skew):
    sequence = jax.random.permutation(own_key, amount)
    packed, common = shares(amount, rows * top, limit, skew, True), shares(amount, rows * top, limit, skew, False)
    places = jnp.arange(amount)

    def named(lengths, rotation):
        used = int((lengths > 0).sum())
        fixed = max(1, used // 4)
        moved = fixed + (places - fixed + rotation * (used - fixed)) % max(1, amount - fixed)
        return jnp.zeros((amount,), jnp.int32).at[sequence[jnp.where(places < fixed, places, moved)]].set(jnp.asarray(lengths, jnp.int32))

    lengths = jnp.where(number % 4 == 0, named(packed, number // 4), named(common, number - number // 4 - 1))
    mixed = jax.random.permutation(jax.random.fold_in(own, 3), amount)
    giver, taker = mixed[0:amount // 2 * 2:2], mixed[1:amount // 2 * 2:2]
    room = jnp.minimum(lengths[giver] - 1, limit - lengths[taker]) // 2
    room = jnp.where((giver == sequence[0]) | (taker == sequence[0]) | (lengths[taker] == 0), 0, jnp.maximum(room, 0))
    moved = jax.random.randint(jax.random.fold_in(own, 4), (amount // 2,), 0, 1 << 20) % (room + 1)
    lengths = lengths.at[giver].add(-moved).at[taker].add(moved)
    members = jnp.searchsorted(jnp.cumsum(lengths), jnp.arange(rows * top), side="right").astype(jnp.int32)
    grid = members.reshape(top, rows).T
    grid = grid[jax.random.permutation(jax.random.fold_in(own, 1), rows)]
    rotation = jax.random.randint(jax.random.fold_in(own, 2), (rows, 1), 0, top)
    return jnp.take_along_axis(grid, (jnp.arange(top)[None, :] + rotation) % top, axis=1)


def shares(amount, total, bound, slope, full):
    loads = [(1 << 20) // math.isqrt(grade ** slope) + 1 for grade in range(1, amount + 1)]
    largest = bound if full else min(bound, max(-(-total // amount), total * loads[0] // sum(loads)))
    least = 1 if total - largest >= amount - 1 else 0
    counts, spare = [largest] + [least] * (amount - 1), total - largest - least * (amount - 1)
    while spare > 0:
        candidates = [i for i in range(1, amount) if counts[i] < largest] or [i for i in range(1, amount) if counts[i] < bound]
        mass, left = sum([loads[i] for i in candidates]), spare
        for i in candidates:
            more = min(bound - counts[i], max(1, left * loads[i] // mass), spare)
            counts[i] = counts[i] + more
            spare = spare - more
    return np.array(counts)


def noise(stream_key, dims, deviation, bound, split=(), held_as=jnp.bfloat16):
    level = shard_levels(stream_key, dims, split, -0.22, 0.18) if split else 1.0
    array = jax.random.normal(stream_key, dims, jnp.float32) * deviation * level
    return jnp.minimum(jnp.maximum(array, -bound), bound).astype(held_as)


def setup_inputs(seed: int = 0) -> dict:
    seeds = jax.random.split(jax.random.key(seed), 7)
    frames = noise(seeds[0], (2, TOKENS, D), 1.0, 6.0, ((0, 2), (1, 128)))
    cotangent = noise(seeds[1], (2, TOKENS, D), 0.5, 3.0, ((0, 2), (1, 128)))
    expert_ids_keys = jax.random.split(jax.random.fold_in(seeds[2], 1), 2 * TOKENS // TOK_DEV)
    expert_ids_turns = jax.random.permutation(jax.random.fold_in(seeds[2], 3), 2 * TOKENS // TOK_DEV)
    expert_ids = jax.vmap(lambda own, number: assign_block(jax.random.fold_in(seeds[2], 2), own, number, TOK_DEV, EXPERTS, TOPK, MOST, 2))(expert_ids_keys, expert_ids_turns).reshape((2, TOKENS, TOPK))
    gate_weights = jnp.clip(jnp.exp(math.log(1.0) - 2.9957323 * jax.random.uniform(seeds[3], (2, TOKENS, TOPK), jnp.float32) ** shard_levels(seeds[3], (2, TOKENS, TOPK), ((0, 2), (1, 128)), -0.2, 0.2)), 0.05, 1.0)
    weight_in = noise(seeds[4], (2, EXPERTS, D, H), D ** -0.5, 0.1875, ((0, 2), (1, 32), (2, 4)))
    weight_out = noise(seeds[5], (2, EXPERTS, H, D), H ** -0.5, 0.21875, ((0, 2), (1, 32), (3, 4)))
    return dict(frames=frames, cotangent=cotangent, expert_ids=expert_ids, gate_weights=gate_weights, weight_in=weight_in, weight_out=weight_out)


def silu_slope(value):
    sigma = jax.nn.sigmoid(value)
    return sigma * (1.0 + value * (1.0 - sigma))


def one_layer(frames, cotangent, expert_ids, gate_weights, weight_in, weight_out):
    groups = N_EXPERT * N_REPLICA
    per_group = TOK_DEV * TOPK
    ids = expert_ids.reshape(groups, per_group)
    onehot = (ids[:, :, None] == jnp.arange(EXPERTS, dtype=jnp.int32)[None, None, :]).astype(jnp.int32)
    position = jnp.sum((jnp.cumsum(onehot, 1) - 1) * onehot, 2).astype(jnp.int32)
    group_index = jnp.arange(groups, dtype=jnp.int32)[:, None]
    column = group_index * MOST + position
    row_flat = group_index * per_group + jnp.arange(per_group, dtype=jnp.int32)[None, :]
    table = jnp.full((EXPERTS, groups * MOST), TOKENS * TOPK, jnp.int32).at[ids, column].set(row_flat)
    padded_x = jnp.concatenate([frames, jnp.zeros((1, D), jnp.bfloat16)], 0)
    padded_g = jnp.concatenate([cotangent, jnp.zeros((1, D), jnp.bfloat16)], 0)
    gate_flat = jnp.concatenate([gate_weights.reshape(-1), jnp.zeros((1,), jnp.float32)], 0)

    def one_expert(carry, inputs):
        rows, w_first, w_second = inputs
        token_rows = rows // TOPK
        inputs_x = padded_x[token_rows]
        slot_grad = (gate_flat[rows][:, None] * padded_g[token_rows].astype(jnp.float32)).astype(jnp.bfloat16)
        pre = jnp.dot(inputs_x, w_first, preferred_element_type=jnp.float32)
        hidden = jax.nn.silu(pre).astype(jnp.bfloat16)
        hidden_grad = jnp.dot(slot_grad, w_second.T, preferred_element_type=jnp.float32)
        pre_grad = (hidden_grad * silu_slope(pre)).astype(jnp.bfloat16)
        row_grad = jnp.dot(pre_grad, w_first.T, preferred_element_type=jnp.float32).astype(jnp.bfloat16)
        carry = carry.at[token_rows].add(row_grad.astype(jnp.float32))
        shaped_x = inputs_x.astype(jnp.float32).reshape(N_EXPERT, N_REPLICA, MOST, D)
        shaped_g = slot_grad.astype(jnp.float32).reshape(N_EXPERT, N_REPLICA, MOST, D)
        shaped_h = hidden.astype(jnp.float32).reshape(N_EXPERT, N_REPLICA, MOST, H)
        shaped_p = pre_grad.astype(jnp.float32).reshape(N_EXPERT, N_REPLICA, MOST, H)
        part_in = jnp.einsum("irmd,irmh->rdh", shaped_x, shaped_p).astype(jnp.bfloat16)
        part_out = jnp.einsum("irmh,irmd->rhd", shaped_h, shaped_g).astype(jnp.bfloat16)
        total_in = jnp.sum(part_in.astype(jnp.float32), 0).astype(jnp.bfloat16)
        total_out = jnp.sum(part_out.astype(jnp.float32), 0).astype(jnp.bfloat16)
        return carry, (total_in, total_out)

    start = jnp.zeros((TOKENS + 1, D), jnp.float32)
    summed, grads = lax.scan(one_expert, start, (table, weight_in, weight_out))
    return summed[:TOKENS].astype(jnp.bfloat16), grads[0], grads[1]


def reference(frames, cotangent, expert_ids, gate_weights, weight_in, weight_out):
    lower = one_layer(frames[0], cotangent[0], expert_ids[0], gate_weights[0], weight_in[0], weight_out[0])
    upper = one_layer(frames[1], cotangent[1], expert_ids[1], gate_weights[1], weight_in[1], weight_out[1])
    sent_grads = jnp.stack([upper[0], lower[0]], 0)
    grad_in = jnp.stack([lower[1], upper[1]], 0)
    grad_out = jnp.stack([lower[2], upper[2]], 0)
    return sent_grads, grad_in, grad_out
```

```python
import jax
import jax.numpy as jnp
from jax import lax
from jax.experimental import pallas as pl
from jax.experimental.pallas import tpu as pltpu
from jax.sharding import PartitionSpec as P

MESH = pl.DeviceIdType.MESH
NZ, NX, NY = 8, 4, 4
FRAMES = 128
D, H = 1024, 768
MOST = 24
PAIR = 2 * MOST
LOCAL = 2
PLANE = NX * LOCAL
ROWS = NZ * NX * MOST
CHUNK = ROWS // 2
QUARTER = D // NY
TILE = 256
COPIES = 128
ORDER = (0, 1, 7, 2, 6, 3, 5, 4)
SLOT = {distance: place for place, distance in enumerate(ORDER)}
PAIRS = len(ORDER) // 2
F32, BF16 = jnp.float32, jnp.bfloat16


def contract(a, b, dim_a, dim_b):
    return lax.dot_general(a, b, (((dim_a,), (dim_b,)), ((), ())), preferred_element_type=F32)


def kernel(
    route_ref,
    x_ref,
    c_ref,
    wi_ref,
    wo_ref,
    sent_ref,
    gi_ref,
    go_ref,
    tok,
    rt,
    hot,
    xs,
    xr,
    wi,
    wo,
    hb,
    pb,
    rg,
    rr,
    par,
    zhalf,
    zin,
    pi,
    po,
    hop_i,
    hop_o,
    end_i,
    end_o,
    fin,
    send_sems,
    recv_sems,
    own_sems,
):
    expert = lax.axis_index("expert")
    z, x = expert // NX, expert % NX
    y, s = lax.axis_index("replica"), lax.axis_index("section")

    def device(dz, dx, dy):
        place = lax.rem(z + dz + NZ, NZ) * NX + lax.rem(x + dx + NX, NX)
        return place, lax.rem(y + dy + NY, NY), s

    z_up, z_down = device(1, 0, 0), device(-1, 0, 0)
    y_up, y_down = device(0, 0, 1), device(0, 0, -1)
    x_far = [device(0, d, 0) for d in range(NX)]
    partner = (expert, y, 1 - s)

    barrier = pltpu.get_barrier_semaphore()
    peers = [z_up, z_down, y_up, y_down, *x_far[1:], partner]
    for peer in peers:
        pl.semaphore_signal(barrier, inc=1, device_id=peer, device_id_type=MESH)
    tok[0, pl.ds(0, FRAMES), :] = x_ref[...]
    tok[1, pl.ds(0, FRAMES), :] = c_ref[...]
    rt[0] = route_ref[...]
    pl.semaphore_wait(barrier, len(peers))

    started = []

    def send(src, dst, to):
        number = len(started)
        copy = pltpu.make_async_remote_copy(
            src_ref=src,
            dst_ref=dst,
            send_sem=send_sems.at[number],
            recv_sem=recv_sems.at[number],
            device_id=to,
            device_id_type=MESH,
        )
        copy.start()
        started.append(copy)
        return copy

    def arrive(copies):
        for copy in copies:
            copy.wait_recv()

    def relay(distance, step, half=None):
        land = (distance + step) % NZ
        to = z_up if step < 0 else z_down
        a, b, size = SLOT[distance] * FRAMES, SLOT[land] * FRAMES, FRAMES
        if half is not None:
            size = FRAMES // 2
            a, b = a + half * size, b + half * size
        copies = []
        if half in (None, 0):
            copies.append(send(rt.at[SLOT[distance]], rt.at[SLOT[land]], to))
        copies.append(send(tok.at[:, pl.ds(a, size)], tok.at[:, pl.ds(b, size)], to))
        return copies

    y_next, y_last = lax.rem(y + 1, NY), lax.rem(y + NY - 1, NY)

    def gather_first(m):
        return [
            send(ref.at[m], full.at[m, y], to)
            for to in (y_up, y_down)
            for ref, full in ((wi_ref, wi), (wo_ref, wo))
        ]

    def gather_second(m, first):
        arrive(first)
        copies = []
        for full, size in ((wi, QUARTER // 2), (wo, H // 2)):
            for place, half, to in ((y_last, 0, y_up), (y_next, 1, y_down)):
                part = full.at[m, place, pl.ds(half * size, size)]
                copies.append(send(part, part, to))
        return copies

    up = relay(0, -1)
    down = relay(0, 1)
    first = [gather_first(m) for m in range(LOCAL)]
    own = []
    for m in range(LOCAL):
        for k, (ref, full) in enumerate(((wi_ref, wi), (wo_ref, wo))):
            own.append(pltpu.make_async_copy(ref.at[m], full.at[m, y], own_sems.at[m, k]))
            own[-1].start()

    earlier = (
        lax.broadcasted_iota(jnp.int32, (FRAMES, FRAMES), 0)
        < lax.broadcasted_iota(jnp.int32, (FRAMES, FRAMES), 1)
    ).astype(BF16)
    place_row = lax.broadcasted_iota(jnp.int32, (PAIR, 2 * FRAMES), 0).astype(F32)
    members = [
        (z * PLANE + lax.rem(x + q // LOCAL, NX) * LOCAL + q % LOCAL).astype(F32)
        for q in range(PLANE)
    ]

    def routing(slot):
        ids, gates = rt[slot, pl.ds(0, 8), :], rt[slot, pl.ds(8, 8), :]
        gate = jnp.concatenate(
            [
                jnp.sum(jnp.where(ids == member, gates, 0.0), 0, keepdims=True)
                for member in members
            ],
            0,
        )
        named = jnp.where(gate > 0.0, 1.0, 0.0)
        place = jnp.dot(named.astype(BF16), earlier, preferred_element_type=F32)
        return gate, jnp.where(gate > 0.0, place, -100.0)

    def pick(p):
        gate_a, place_a = routing(2 * p)
        gate_b, place_b = routing(2 * p + 1)
        gate = jnp.concatenate([gate_a, gate_b], 1)
        place = jnp.concatenate([place_a, place_b + float(MOST)], 1)
        slot_gates = []
        for q in range(PLANE):
            match = place_row == place[q : q + 1, :]
            hot[p, pl.ds(q * PAIR, PAIR), :] = jnp.where(match, 1.0, 0.0).astype(BF16)
            slot_gates.append(
                jnp.sum(jnp.where(match, gate[q : q + 1, :], 0.0), 1, keepdims=True)
            )
        slot_gate = jnp.concatenate(slot_gates, 0)
        source = pl.ds(p * 2 * FRAMES, 2 * FRAMES)
        for kind in range(2):
            for n in range(D // TILE):
                columns = pl.ds(n * TILE, TILE)
                rows = jnp.dot(hot[p], tok[kind, source, columns], preferred_element_type=F32)
                if kind:
                    rows = rows * slot_gate
                rows = rows.astype(BF16)
                for q in range(PLANE):
                    d, m = q // LOCAL, q % LOCAL
                    block = rows[q * PAIR : (q + 1) * PAIR, :]
                    if d:
                        xs[p, m, d - 1, kind, :, columns] = block
                    else:
                        xr[m, kind, pl.ds(p * NX * PAIR, PAIR), columns] = block

    def scatter(p, m):
        copies = []
        for d in range(1, NX):
            rows = pl.ds((p * NX + NX - d) * PAIR, PAIR)
            copies.append(send(xs.at[p, m, d - 1], xr.at[m, :, rows], x_far[d]))
        return copies

    rows_in = {}
    arrive(up)
    up = relay(7, -1)
    arrive(down)
    down = relay(1, 1)
    pick(0)
    rows_in[0, 0] = scatter(0, 0)
    rows_in[0, 1] = scatter(0, 1)
    arrive(up)
    up = relay(6, -1)
    arrive(down)
    down = relay(2, 1)
    pick(1)
    rows_in[1, 0] = scatter(1, 0)
    second = [gather_second(0, first[0])]
    arrive(up)
    up = relay(5, -1, 0)
    arrive(down)
    down = relay(3, 1, 1)
    pick(2)
    rows_in[2, 0] = scatter(2, 0)
    second.append(gather_second(1, first[1]))
    arrive(up)
    arrive(down)
    pick(3)
    rows_in[3, 0] = scatter(3, 0)
    for p in range(1, PAIRS):
        rows_in[p, 1] = scatter(p, 1)

    def forward(m, c):
        rows = pl.ds(c * CHUNK, CHUNK)

        @pl.loop(0, H // TILE)
        def _(n):
            columns = pl.ds(pl.multiple_of(n * TILE, TILE), TILE)
            pre = jnp.zeros((CHUNK, TILE), F32)
            hidden_grad = jnp.zeros((CHUNK, TILE), F32)
            for r in range(NY):
                part = pl.ds(r * QUARTER, QUARTER)
                pre += contract(xr[m, 0, rows, part], wi[m, r, :, columns], 1, 0)
                hidden_grad += contract(xr[m, 1, rows, part], wo[m, r, columns, :], 1, 1)
            sigma = jax.nn.sigmoid(pre)
            slope = sigma * (1.0 + pre * (1.0 - sigma))
            hb[columns, rows] = jnp.transpose(pre * sigma).astype(BF16)
            pb[rows, columns] = (hidden_grad * slope).astype(BF16)

    def backward(m, c):
        rows = pl.ds(c * CHUNK, CHUNK)

        @pl.loop(0, NY)
        def _(r):
            columns = pl.ds(pl.multiple_of(r * QUARTER, QUARTER), QUARTER)
            rg[m, rows, columns] = contract(pb[rows, :], wi[m, r], 1, 1).astype(BF16)

    def parts(m, j):
        columns = pl.ds(pl.multiple_of(lax.rem(y + j, NY) * QUARTER, QUARTER), QUARTER)
        pi[m, j] = contract(xr[m, 0, :, columns], pb[...], 0, 0).astype(BF16)
        po[m, j] = contract(hb[...], xr[m, 1, :, columns], 1, 0).astype(BF16)

    half_i, half_o = QUARTER // 2, H // 2

    def reduce_first(m):
        copies = []
        for way, to in ((0, y_up), (1, y_down)):
            copies.append(send(pi.at[m, 2, pl.ds(way * half_i, half_i)], hop_i.at[m, way], to))
            copies.append(send(po.at[m, 2, pl.ds(way * half_o, half_o)], hop_o.at[m, way], to))
        return copies

    def add(ref, place, term):
        ref[place] = (ref[place].astype(F32) + term.astype(F32)).astype(BF16)

    def reduce_second(m, copies):
        after = []
        for way, to in ((0, y_up), (1, y_down)):
            j = 1 if way == 0 else 3
            arrive(copies[2 * way : 2 * way + 2])
            add(pi, (m, j, pl.ds(way * half_i, half_i)), hop_i[m, way])
            add(po, (m, j, pl.ds(way * half_o, half_o)), hop_o[m, way])
            after.append(send(pi.at[m, j], end_i.at[m, way], to))
            after.append(send(po.at[m, j], end_o.at[m, way], to))
        return after

    def reduce_last(m, copies):
        arrive(copies)
        for out, part, end in ((gi_ref, pi, end_i), (go_ref, po, end_o)):
            total = part[m, 0].astype(F32) + end[m, 0].astype(F32) + end[m, 1].astype(F32)
            out[m] = total.astype(BF16)

    def rows_back(p, m):
        copies = []
        for b in range(1, NX):
            rows = pl.ds((p * NX + b) * PAIR, PAIR)
            place = pl.ds(((NX - b) * LOCAL + m) * PAIR, PAIR)
            copies.append(send(rg.at[m, rows], rr.at[p, place], x_far[b]))
        rr[p, pl.ds(m * PAIR, PAIR), :] = rg[m, pl.ds(p * NX * PAIR, PAIR), :]
        return copies

    def combine(p):
        for n in range(D // TILE):
            columns = pl.ds(n * TILE, TILE)
            total = contract(hot[p], rr[p, :, columns], 0, 0)
            par[pl.ds(p * 2 * FRAMES, 2 * FRAMES), columns] = total.astype(BF16)

    arrive(second[0])
    own[0].wait()
    own[1].wait()
    for c in range(2):
        for p in (2 * c, 2 * c + 1):
            arrive(rows_in[p, 0])
        forward(0, c)
    parts(0, 2)
    sums = [reduce_first(0)]
    parts(0, 1)
    parts(0, 3)
    parts(0, 0)
    for c in range(2):
        backward(0, c)
    sums[0] = reduce_second(0, sums[0])

    arrive(second[1])
    own[2].wait()
    own[3].wait()
    for c in range(2):
        for p in (2 * c, 2 * c + 1):
            arrive(rows_in[p, 1])
        if c == 1:
            back = {(p, 0): rows_back(p, 0) for p in reversed(range(PAIRS))}
        forward(1, c)
    parts(1, 2)
    sums.append(reduce_first(1))
    parts(1, 1)
    parts(1, 3)
    for c in (1, 0):
        backward(1, c)
        for p in (2 * c + 1, 2 * c):
            back[p, 1] = rows_back(p, 1)
    parts(1, 0)
    sums[1] = reduce_second(1, sums[1])
    reduce_last(0, sums[0])

    def chunk(distance, half=None):
        start, size = SLOT[distance] * FRAMES, FRAMES
        if half is not None:
            size = FRAMES // 2
            start += half * size
        return pl.ds(start, size)

    def returned(p):
        arrive(back[p, 0] + back[p, 1])
        combine(p)

    returned(3)
    up = send(par.at[chunk(4, 0)], zhalf.at[0], z_up)
    down = send(par.at[chunk(4, 1)], zhalf.at[1], z_down)
    returned(2)
    arrive([up])
    add(par, (chunk(3, 0),), zhalf[0])
    up = send(par.at[chunk(3)], zin.at[0, 0], z_up)
    arrive([down])
    add(par, (chunk(5, 1),), zhalf[1])
    down = send(par.at[chunk(5)], zin.at[1, 0], z_down)
    returned(1)
    for step, (a, b) in enumerate(((2, 6), (1, 7))):
        if step == 1:
            returned(0)
        arrive([up])
        add(par, (chunk(a),), zin[0, step])
        up = send(par.at[chunk(a)], zin.at[0, step + 1], z_up)
        arrive([down])
        add(par, (chunk(b),), zin[1, step])
        down = send(par.at[chunk(b)], zin.at[1, step + 1], z_down)
    arrive([up, down])
    total = par[chunk(0), :].astype(F32) + zin[0, 2].astype(F32) + zin[1, 2].astype(F32)
    fin[...] = total.astype(BF16)
    last = send(fin, sent_ref, partner)
    reduce_last(1, sums[1])
    arrive([last])
    for copy in started:
        copy.wait_send()


def per_device(frames, cotangent, expert_ids, gate_weights, weight_in, weight_out):
    route = jnp.concatenate([expert_ids[0].astype(F32).T, gate_weights[0].T], 0)
    vmem = pl.BlockSpec(memory_space=pltpu.VMEM)
    anywhere = pl.BlockSpec(memory_space=pl.ANY)
    sent, grad_in, grad_out = pl.pallas_call(
        kernel,
        name="relay",
        out_shape=(
            jax.ShapeDtypeStruct((FRAMES, D), BF16),
            jax.ShapeDtypeStruct((LOCAL, QUARTER, H), BF16),
            jax.ShapeDtypeStruct((LOCAL, H, QUARTER), BF16),
        ),
        in_specs=[vmem, vmem, vmem, anywhere, anywhere],
        out_specs=(anywhere, vmem, vmem),
        scratch_shapes=[
            pltpu.VMEM((2, NZ * FRAMES, D), BF16),
            pltpu.VMEM((NZ, 16, FRAMES), F32),
            pltpu.VMEM((PAIRS, PLANE * PAIR, 2 * FRAMES), BF16),
            pltpu.VMEM((PAIRS, LOCAL, NX - 1, 2, PAIR, D), BF16),
            pltpu.VMEM((LOCAL, 2, ROWS, D), BF16),
            pltpu.VMEM((LOCAL, NY, QUARTER, H), BF16),
            pltpu.VMEM((LOCAL, NY, H, QUARTER), BF16),
            pltpu.VMEM((H, ROWS), BF16),
            pltpu.VMEM((ROWS, H), BF16),
            pltpu.VMEM((LOCAL, ROWS, D), BF16),
            pltpu.VMEM((PAIRS, PLANE * PAIR, D), BF16),
            pltpu.VMEM((NZ * FRAMES, D), BF16),
            pltpu.VMEM((2, FRAMES // 2, D), BF16),
            pltpu.VMEM((2, 3, FRAMES, D), BF16),
            pltpu.VMEM((LOCAL, NY, QUARTER, H), BF16),
            pltpu.VMEM((LOCAL, NY, H, QUARTER), BF16),
            pltpu.VMEM((LOCAL, 2, QUARTER // 2, H), BF16),
            pltpu.VMEM((LOCAL, 2, H // 2, QUARTER), BF16),
            pltpu.VMEM((LOCAL, 2, QUARTER, H), BF16),
            pltpu.VMEM((LOCAL, 2, H, QUARTER), BF16),
            pltpu.VMEM((FRAMES, D), BF16),
            pltpu.SemaphoreType.DMA((COPIES,)),
            pltpu.SemaphoreType.DMA((COPIES,)),
            pltpu.SemaphoreType.DMA((LOCAL, 2)),
        ],
        compiler_params=pltpu.CompilerParams(
            collective_id=0, has_side_effects=True, vmem_limit_bytes=60 * 2**20
        ),
    )(route, frames[0], cotangent[0], weight_in[0], weight_out[0])
    return sent[None], grad_in[None], grad_out[None]


def solution(mesh):
    rows = P("section", ("expert", "replica"), None)
    first = P("section", "expert", "replica", None)
    second = P("section", "expert", None, "replica")
    return jax.shard_map(
        per_device,
        mesh=mesh,
        in_specs=(rows, rows, rows, rows, first, second),
        out_specs=(rows, first, second),
        check_vma=False,
    )
```

```python
import jax
import jax.numpy as jnp
from jax import lax
from jax.experimental import pallas as pl
from jax.experimental.pallas import tpu as pltpu
from jax.sharding import PartitionSpec as P

MESH = pl.DeviceIdType.MESH
NZ, NX, NY = 8, 4, 4
FRAMES = 128
D, H = 1024, 768
MOST = 24
PAIR = 2 * MOST
LOCAL = 2
PLANE = NX * LOCAL
ROWS = NZ * NX * MOST
CHUNK = ROWS // 2
QUARTER = D // NY
TILE = 256
COPIES = 176
HALVES = ((0, D // 2), (D // 2, D // 2))
ORDER = (0, 1, 7, 2, 6, 3, 5, 4)
SLOT = {distance: place for place, distance in enumerate(ORDER)}
PAIRS = len(ORDER) // 2
F32, BF16 = jnp.float32, jnp.bfloat16


def contract(a, b, dim_a, dim_b):
    return lax.dot_general(a, b, (((dim_a,), (dim_b,)), ((), ())), preferred_element_type=F32)


def kernel(
    ids_ref,
    gate_ref,
    x_ref,
    c_ref,
    wi_ref,
    wo_ref,
    sent_ref,
    gi_ref,
    go_ref,
    tok,
    rt,
    hot,
    xs,
    xr,
    wi,
    wo,
    hb,
    pb,
    rg,
    rr,
    par,
    zhalf,
    zin,
    pi,
    po,
    hop_i,
    hop_o,
    end_i,
    end_o,
    fin,
    send_sems,
    recv_sems,
    own_sems,
):
    expert = lax.axis_index("expert")
    z, x = expert // NX, expert % NX
    y, s = lax.axis_index("replica"), lax.axis_index("section")

    def device(dz, dx, dy):
        place = lax.rem(z + dz + NZ, NZ) * NX + lax.rem(x + dx + NX, NX)
        return place, lax.rem(y + dy + NY, NY), s

    z_up, z_down = device(1, 0, 0), device(-1, 0, 0)
    y_up, y_down = device(0, 0, 1), device(0, 0, -1)
    x_far = [device(0, d, 0) for d in range(NX)]
    partner = (expert, y, 1 - s)

    barrier = pltpu.get_barrier_semaphore()
    peers = [z_up, z_down, y_up, y_down, *x_far[1:], partner]
    for peer in peers:
        pl.semaphore_signal(barrier, inc=1, device_id=peer, device_id_type=MESH)
    tok[0, pl.ds(0, FRAMES), :] = x_ref[...]
    tok[1, pl.ds(0, FRAMES), :] = c_ref[...]
    rt[0, pl.ds(0, 8), :] = ids_ref[...].astype(F32)
    rt[0, pl.ds(8, 8), :] = gate_ref[...]
    pl.semaphore_wait(barrier, len(peers))

    started = []

    def send(src, dst, to):
        number = len(started)
        copy = pltpu.make_async_remote_copy(
            src_ref=src,
            dst_ref=dst,
            send_sem=send_sems.at[number],
            recv_sem=recv_sems.at[number],
            device_id=to,
            device_id_type=MESH,
        )
        copy.start()
        started.append(copy)
        return copy

    def arrive(copies):
        for copy in copies:
            copy.wait_recv()

    def hop_route(distance, step):
        to = z_up if step < 0 else z_down
        return [send(rt.at[SLOT[distance]], rt.at[SLOT[(distance + step) % NZ]], to)]

    def hop(distance, step, kind, half=None, columns=(0, D)):
        land = (distance + step) % NZ
        to = z_up if step < 0 else z_down
        a, b, size = SLOT[distance] * FRAMES, SLOT[land] * FRAMES, FRAMES
        if half is not None:
            size = FRAMES // 2
            a, b = a + half * size, b + half * size
        columns = pl.ds(*columns)
        return [send(tok.at[kind, pl.ds(a, size), columns], tok.at[kind, pl.ds(b, size), columns], to)]

    y_next, y_last = lax.rem(y + 1, NY), lax.rem(y + NY - 1, NY)

    def gather_first(m):
        return [
            send(ref.at[m], full.at[m, y], to)
            for to in (y_up, y_down)
            for ref, full in ((wi_ref, wi), (wo_ref, wo))
        ]

    def gather_second(m, first):
        arrive(first)
        copies = []
        for full, size in ((wi, QUARTER // 2), (wo, H // 2)):
            for place, half, to in ((y_last, 0, y_up), (y_next, 1, y_down)):
                part = full.at[m, place, pl.ds(half * size, size)]
                copies.append(send(part, part, to))
        return copies

    up_route, down_route = hop_route(0, -1), hop_route(0, 1)
    up, down = {}, {}
    for kind in range(2):
        for columns in HALVES:
            down[kind, columns] = hop(0, 1, kind, None, columns)
            up[kind, columns] = hop(0, -1, kind, None, columns)
    first = [gather_first(0)]
    own = []
    for m in range(LOCAL):
        for k, (ref, full) in enumerate(((wi_ref, wi), (wo_ref, wo))):
            own.append(pltpu.make_async_copy(ref.at[m], full.at[m, y], own_sems.at[m, k]))
            own[-1].start()

    earlier = (
        lax.broadcasted_iota(jnp.int32, (FRAMES, FRAMES), 0)
        < lax.broadcasted_iota(jnp.int32, (FRAMES, FRAMES), 1)
    ).astype(BF16)
    place_row = lax.broadcasted_iota(jnp.int32, (PAIR, 2 * FRAMES), 0).astype(F32)
    members = [
        (z * PLANE + lax.rem(x + q // LOCAL, NX) * LOCAL + q % LOCAL).astype(F32)
        for q in range(PLANE)
    ]

    def routing(slot):
        ids, gates = rt[slot, pl.ds(0, 8), :], rt[slot, pl.ds(8, 8), :]
        gate = jnp.concatenate(
            [
                jnp.sum(jnp.where(ids == member, gates, 0.0), 0, keepdims=True)
                for member in members
            ],
            0,
        )
        named = jnp.where(gate > 0.0, 1.0, 0.0)
        place = jnp.dot(named.astype(BF16), earlier, preferred_element_type=F32)
        return gate, jnp.where(gate > 0.0, place, -100.0)

    def prepare(p):
        gate_a, place_a = routing(2 * p)
        gate_b, place_b = routing(2 * p + 1)
        gate = jnp.concatenate([gate_a, gate_b], 1)
        place = jnp.concatenate([place_a, place_b + float(MOST)], 1)
        slot_gates = []
        for q in range(PLANE):
            match = place_row == place[q : q + 1, :]
            hot[p, pl.ds(q * PAIR, PAIR), :] = jnp.where(match, 1.0, 0.0).astype(BF16)
            slot_gates.append(
                jnp.sum(jnp.where(match, gate[q : q + 1, :], 0.0), 1, keepdims=True)
            )
        return jnp.concatenate(slot_gates, 0)

    def pick(p, kind, slot_gate, columns=(0, D)):
        source = pl.ds(p * 2 * FRAMES, 2 * FRAMES)
        for start in range(columns[0], columns[0] + columns[1], TILE):
            tile = pl.ds(start, TILE)
            rows = jnp.dot(hot[p], tok[kind, source, tile], preferred_element_type=F32)
            if kind:
                rows = rows * slot_gate
            rows = rows.astype(BF16)
            for q in range(PLANE):
                d, m = q // LOCAL, q % LOCAL
                block = rows[q * PAIR : (q + 1) * PAIR, :]
                if d:
                    xs[p, m, d - 1, kind, :, tile] = block
                else:
                    xr[m, kind, pl.ds(p * NX * PAIR, PAIR), tile] = block

    rows_in = {(p, m): [] for p in range(PAIRS) for m in range(LOCAL)}

    def scatter(p, m, kind, columns=(0, D)):
        columns = pl.ds(*columns)
        for d in range(1, NX):
            rows = pl.ds((p * NX + NX - d) * PAIR, PAIR)
            rows_in[p, m].append(
                send(xs.at[p, m, d - 1, kind, :, columns], xr.at[m, kind, rows, columns], x_far[d])
            )

    arrive(down_route)
    down_route = hop_route(1, 1)
    slot_gate = prepare(0)
    arrive(up_route)
    up_route = hop_route(7, -1)
    up_next, down_next = {}, {}
    for kind in range(2):
        for place, columns in enumerate(HALVES):
            arrive(down[kind, columns])
            if place == len(HALVES) - 1:
                down_next[kind] = hop(1, 1, kind)
                for part in HALVES:
                    arrive(up[kind, part])
                up_next[kind] = hop(7, -1, kind)
            pick(0, kind, slot_gate, columns)
            for m in range(LOCAL):
                scatter(0, m, kind, columns)
    up, down = up_next, down_next
    for p, (a, b) in ((1, (6, 2)), (2, (5, 3))):
        if p == 2:
            second = [gather_second(0, first[0])]
            first.append(gather_first(1))
        arrive(down_route)
        arrive(up_route)
        if p == 1:
            down_route = hop_route(b, 1)
        up_route = hop_route(a, -1)
        slot_gate = prepare(p)
        up_next, down_next = {}, {}
        for kind in range(2):
            arrive(down[kind])
            down_next[kind] = hop(b, 1, kind, 1 if p == 2 else None)
            arrive(up[kind])
            up_next[kind] = hop(a, -1, kind, 0 if p == 2 else None)
            pick(p, kind, slot_gate)
            scatter(p, 0, kind)
        up, down = up_next, down_next
    arrive(up_route)
    slot_gate = prepare(3)
    for kind in range(2):
        arrive(down[kind] + up[kind])
        pick(3, kind, slot_gate)
        scatter(3, 0, kind)
    for p in range(1, PAIRS):
        for kind in range(2):
            scatter(p, 1, kind)

    def forward(m, c):
        rows = pl.ds(c * CHUNK, CHUNK)

        @pl.loop(0, H // TILE)
        def _(n):
            columns = pl.ds(pl.multiple_of(n * TILE, TILE), TILE)
            pre = jnp.zeros((CHUNK, TILE), F32)
            hidden_grad = jnp.zeros((CHUNK, TILE), F32)
            for r in range(NY):
                part = pl.ds(r * QUARTER, QUARTER)
                pre += contract(xr[m, 0, rows, part], wi[m, r, :, columns], 1, 0)
                hidden_grad += contract(xr[m, 1, rows, part], wo[m, r, columns, :], 1, 1)
            sigma = jax.nn.sigmoid(pre)
            slope = sigma * (1.0 + pre * (1.0 - sigma))
            hb[columns, rows] = jnp.transpose(pre * sigma).astype(BF16)
            pb[rows, columns] = (hidden_grad * slope).astype(BF16)

    def backward(m, c):
        rows = pl.ds(c * CHUNK, CHUNK)

        @pl.loop(0, NY)
        def _(r):
            columns = pl.ds(pl.multiple_of(r * QUARTER, QUARTER), QUARTER)
            rg[m, rows, columns] = contract(pb[rows, :], wi[m, r], 1, 1).astype(BF16)

    def parts(m, j):
        columns = pl.ds(pl.multiple_of(lax.rem(y + j, NY) * QUARTER, QUARTER), QUARTER)
        pi[m, j] = contract(xr[m, 0, :, columns], pb[...], 0, 0).astype(BF16)
        po[m, j] = contract(hb[...], xr[m, 1, :, columns], 1, 0).astype(BF16)

    half_i, half_o = QUARTER // 2, H // 2

    def reduce_first(m):
        copies = []
        for way, to in ((0, y_up), (1, y_down)):
            copies.append(send(pi.at[m, 2, pl.ds(way * half_i, half_i)], hop_i.at[m, way], to))
            copies.append(send(po.at[m, 2, pl.ds(way * half_o, half_o)], hop_o.at[m, way], to))
        return copies

    def add(ref, place, term):
        ref[place] = (ref[place].astype(F32) + term.astype(F32)).astype(BF16)

    def reduce_second(m, copies):
        after = []
        for way, to in ((0, y_up), (1, y_down)):
            j = 1 if way == 0 else 3
            arrive(copies[2 * way : 2 * way + 2])
            add(pi, (m, j, pl.ds(way * half_i, half_i)), hop_i[m, way])
            add(po, (m, j, pl.ds(way * half_o, half_o)), hop_o[m, way])
            after.append(send(pi.at[m, j], end_i.at[m, way], to))
            after.append(send(po.at[m, j], end_o.at[m, way], to))
        return after

    def reduce_last(m, copies):
        arrive(copies)
        for out, part, end in ((gi_ref, pi, end_i), (go_ref, po, end_o)):
            total = part[m, 0].astype(F32) + end[m, 0].astype(F32) + end[m, 1].astype(F32)
            out[m] = total.astype(BF16)

    back = {(p, columns): [] for p in range(PAIRS) for columns in ((0, D), *HALVES)}

    def rows_back(p, m, columns=(0, D)):
        part = pl.ds(*columns)
        for b in range(1, NX):
            rows = pl.ds((p * NX + b) * PAIR, PAIR)
            place = pl.ds(((NX - b) * LOCAL + m) * PAIR, PAIR)
            back[p, columns].append(send(rg.at[m, rows, part], rr.at[p, place, part], x_far[b]))
        rr[p, pl.ds(m * PAIR, PAIR), part] = rg[m, pl.ds(p * NX * PAIR, PAIR), part]

    def combine(p, columns):
        for start in range(columns[0], columns[0] + columns[1], TILE):
            tile = pl.ds(start, TILE)
            total = contract(hot[p], rr[p, :, tile], 0, 0)
            par[pl.ds(p * 2 * FRAMES, 2 * FRAMES), tile] = total.astype(BF16)

    arrive(second[0])
    own[0].wait()
    own[1].wait()
    for c in range(2):
        for p in (2 * c, 2 * c + 1):
            arrive(rows_in[p, 0])
        forward(0, c)
    parts(0, 2)
    sums = [reduce_first(0)]
    second.append(gather_second(1, first[1]))
    parts(0, 1)
    parts(0, 3)
    parts(0, 0)
    for c in range(2):
        backward(0, c)
    sums[0] = reduce_second(0, sums[0])

    arrive(second[1])
    own[2].wait()
    own[3].wait()
    arrive(rows_in[0, 1] + rows_in[1, 1])
    forward(1, 0)
    backward(1, 0)
    arrive(rows_in[2, 1] + rows_in[3, 1])
    rows_back(3, 0)
    rows_back(2, 0)
    forward(1, 1)
    parts(1, 2)
    sums.append(reduce_first(1))
    backward(1, 1)
    rows_back(3, 1)
    rows_back(2, 1)
    rows_back(1, 0)
    rows_back(1, 1)
    for columns in HALVES:
        for m in range(LOCAL):
            rows_back(0, m, columns)
    parts(1, 1)
    parts(1, 3)
    parts(1, 0)
    reduce_last(0, sums[0])

    def chunk(distance, half=None):
        start, size = SLOT[distance] * FRAMES, FRAMES
        if half is not None:
            size = FRAMES // 2
            start += half * size
        return pl.ds(start, size)

    def returned(p, columns=(0, D)):
        arrive(back[p, columns])
        combine(p, columns)

    returned(3)
    up = send(par.at[chunk(4, 0)], zhalf.at[0], z_up)
    down = send(par.at[chunk(4, 1)], zhalf.at[1], z_down)
    sums[1] = reduce_second(1, sums[1])
    returned(2)
    arrive([up])
    add(par, (chunk(3, 0),), zhalf[0])
    up = send(par.at[chunk(3)], zin.at[0, 0], z_up)
    arrive([down])
    add(par, (chunk(5, 1),), zhalf[1])
    down = send(par.at[chunk(5)], zin.at[1, 0], z_down)
    returned(1)
    arrive([up])
    add(par, (chunk(2),), zin[0, 0])
    up = send(par.at[chunk(2)], zin.at[0, 1], z_up)
    arrive([down])
    add(par, (chunk(6),), zin[1, 0])
    down = send(par.at[chunk(6)], zin.at[1, 1], z_down)
    ends = []
    for place, columns in enumerate(HALVES):
        part = pl.ds(*columns)
        returned(0, columns)
        if place == 0:
            arrive([down, up])
        add(par, (chunk(7), part), zin[1, 1, :, part])
        ends.append([send(par.at[chunk(7), part], zin.at[1, 2, :, part], z_down)])
        add(par, (chunk(1), part), zin[0, 1, :, part])
        ends[-1].append(send(par.at[chunk(1), part], zin.at[0, 2, :, part], z_up))
    last = []
    for end, columns in zip(ends, HALVES):
        part = pl.ds(*columns)
        arrive(end)
        total = par[chunk(0), part].astype(F32)
        total = total + zin[0, 2, :, part].astype(F32) + zin[1, 2, :, part].astype(F32)
        fin[:, part] = total.astype(BF16)
        last.append(send(fin.at[:, part], sent_ref.at[:, part], partner))
    reduce_last(1, sums[1])
    arrive(last)
    for copy in started:
        copy.wait_send()


def publish(sent_in, gi_in, go_in, sent_out, gi_out, go_out, sent_held, gi_held, go_held, sems):
    trios = []
    for m in range(LOCAL):
        trios.append((gi_in.at[m], gi_held.at[m], gi_out.at[m]))
        trios.append((go_in.at[m], go_held.at[m], go_out.at[m]))
    trios.append((sent_in, sent_held, sent_out))
    inward = [pltpu.make_async_copy(a, h, sems.at[0, i]) for i, (a, h, _) in enumerate(trios)]
    outward = [pltpu.make_async_copy(h, b, sems.at[1, i]) for i, (_, h, b) in enumerate(trios)]
    for copy in inward:
        copy.start()
    for arriving, leaving in zip(inward, outward):
        arriving.wait()
        leaving.start()
    for copy in outward:
        copy.wait()


def per_device(frames, cotangent, expert_ids, gate_weights, weight_in, weight_out):
    vmem = pl.BlockSpec(memory_space=pltpu.VMEM)
    anywhere = pl.BlockSpec(memory_space=pl.ANY)
    shapes = (
        jax.ShapeDtypeStruct((FRAMES, D), BF16),
        jax.ShapeDtypeStruct((LOCAL, QUARTER, H), BF16),
        jax.ShapeDtypeStruct((LOCAL, H, QUARTER), BF16),
    )
    results = pl.pallas_call(
        kernel,
        name="relay",
        out_shape=shapes,
        in_specs=[vmem, vmem, vmem, vmem, anywhere, anywhere],
        out_specs=(anywhere, vmem, vmem),
        scratch_shapes=[
            pltpu.VMEM((2, NZ * FRAMES, D), BF16),
            pltpu.VMEM((NZ, 16, FRAMES), F32),
            pltpu.VMEM((PAIRS, PLANE * PAIR, 2 * FRAMES), BF16),
            pltpu.VMEM((PAIRS, LOCAL, NX - 1, 2, PAIR, D), BF16),
            pltpu.VMEM((LOCAL, 2, ROWS, D), BF16),
            pltpu.VMEM((LOCAL, NY, QUARTER, H), BF16),
            pltpu.VMEM((LOCAL, NY, H, QUARTER), BF16),
            pltpu.VMEM((H, ROWS), BF16),
            pltpu.VMEM((ROWS, H), BF16),
            pltpu.VMEM((LOCAL, ROWS, D), BF16),
            pltpu.VMEM((PAIRS, PLANE * PAIR, D), BF16),
            pltpu.VMEM((NZ * FRAMES, D), BF16),
            pltpu.VMEM((2, FRAMES // 2, D), BF16),
            pltpu.VMEM((2, 3, FRAMES, D), BF16),
            pltpu.VMEM((LOCAL, NY, QUARTER, H), BF16),
            pltpu.VMEM((LOCAL, NY, H, QUARTER), BF16),
            pltpu.VMEM((LOCAL, 2, QUARTER // 2, H), BF16),
            pltpu.VMEM((LOCAL, 2, H // 2, QUARTER), BF16),
            pltpu.VMEM((LOCAL, 2, QUARTER, H), BF16),
            pltpu.VMEM((LOCAL, 2, H, QUARTER), BF16),
            pltpu.VMEM((FRAMES, D), BF16),
            pltpu.SemaphoreType.DMA((COPIES,)),
            pltpu.SemaphoreType.DMA((COPIES,)),
            pltpu.SemaphoreType.DMA((LOCAL, 2)),
        ],
        compiler_params=pltpu.CompilerParams(
            collective_id=0, has_side_effects=True, vmem_limit_bytes=60 * 2**20
        ),
    )(expert_ids[0].T, gate_weights[0].T, frames[0], cotangent[0], weight_in[0], weight_out[0])
    sent, grad_in, grad_out = pl.pallas_call(
        publish,
        name="publish",
        out_shape=shapes,
        in_specs=[anywhere] * 3,
        out_specs=(anywhere,) * 3,
        scratch_shapes=[
            *[pltpu.VMEM(shape.shape, shape.dtype) for shape in shapes],
            pltpu.SemaphoreType.DMA((2, 1 + 2 * LOCAL)),
        ],
    )(*results)
    return sent[None], grad_in[None], grad_out[None]


def solution(mesh):
    rows = P("section", ("expert", "replica"), None)
    first = P("section", "expert", "replica", None)
    second = P("section", "expert", None, "replica")
    return jax.shard_map(
        per_device,
        mesh=mesh,
        in_specs=(rows, rows, rows, rows, first, second),
        out_specs=(rows, first, second),
        check_vma=False,
    )
```

```python
import jax
import jax.numpy as jnp
from jax import lax
from jax.experimental import pallas as pl
from jax.experimental.pallas import tpu as pltpu
from jax.sharding import PartitionSpec as P

MESH = pl.DeviceIdType.MESH
NZ, NX, NY = 8, 4, 4
FRAMES = 128
D, H = 1024, 768
MOST = 24
PAIR = 2 * MOST
LOCAL = 2
PLANE = NX * LOCAL
ROWS = NZ * NX * MOST
CHUNK = ROWS // 2
QUARTER = D // NY
TILE = 256
COPIES = 176
EARLY = 16
ORDER = (0, 1, 7, 2, 6, 3, 5, 4)
SLOT = {distance: place for place, distance in enumerate(ORDER)}
PAIRS = len(ORDER) // 2
F32, BF16 = jnp.float32, jnp.bfloat16


def contract(a, b, dim_a, dim_b):
    return lax.dot_general(a, b, (((dim_a,), (dim_b,)), ((), ())), preferred_element_type=F32)


def kernel(
    ids_ref,
    gate_ref,
    x_ref,
    c_ref,
    wi_ref,
    wo_ref,
    sent_ref,
    gi_ref,
    go_ref,
    tok,
    rt,
    hot,
    xs,
    xr,
    wi,
    wo,
    hb,
    pb,
    rg,
    rr,
    par,
    zhalf,
    zin,
    pi,
    po,
    hop_i,
    hop_o,
    end_i,
    end_o,
    fin,
    ids_held,
    send_sems,
    recv_sems,
    own_sems,
    local_sems,
):
    expert = lax.axis_index("expert")
    z, x = expert // NX, expert % NX
    y, s = lax.axis_index("replica"), lax.axis_index("section")

    def device(dz, dx, dy):
        place = lax.rem(z + dz + NZ, NZ) * NX + lax.rem(x + dx + NX, NX)
        return place, lax.rem(y + dy + NY, NY), s

    z_up, z_down = device(1, 0, 0), device(-1, 0, 0)
    y_up, y_down = device(0, 0, 1), device(0, 0, -1)
    x_far = [device(0, d, 0) for d in range(NX)]
    partner = (expert, y, 1 - s)

    z_up_other, z_down_other = (*z_up[:2], 1 - s), (*z_down[:2], 1 - s)
    barrier = pltpu.get_barrier_semaphore()
    peers = [z_up, z_down, y_up, y_down, *x_far[1:], partner, z_up_other, z_down_other]
    for peer in peers:
        pl.semaphore_signal(barrier, inc=1, device_id=peer, device_id_type=MESH)
    inputs = [
        pltpu.make_async_copy(src, dst, local_sems.at[i])
        for i, (src, dst) in enumerate(
            (
                (ids_ref, ids_held),
                (gate_ref, rt.at[0, pl.ds(8, 8)]),
                (x_ref, tok.at[0, pl.ds(0, FRAMES)]),
                (c_ref, tok.at[1, pl.ds(0, FRAMES)]),
            )
        )
    ]
    for copy in inputs:
        copy.start()

    started = []

    def send(src, dst, to):
        number = len(started)
        copy = pltpu.make_async_remote_copy(
            src_ref=src,
            dst_ref=dst,
            send_sem=send_sems.at[number],
            recv_sem=recv_sems.at[number],
            device_id=to,
            device_id_type=MESH,
        )
        copy.start()
        started.append(copy)
        return copy

    def arrive(copies):
        for copy in copies:
            copy.wait_recv()

    def hop_route(distance, step):
        to = z_up if step < 0 else z_down
        return [send(rt.at[SLOT[distance]], rt.at[SLOT[(distance + step) % NZ]], to)]

    def hop(distance, step, kind, half=None):
        land = (distance + step) % NZ
        to = z_up if step < 0 else z_down
        a, b, size = SLOT[distance] * FRAMES, SLOT[land] * FRAMES, FRAMES
        if half is not None:
            size = FRAMES // 2
            a, b = a + half * size, b + half * size
        return [send(tok.at[kind, pl.ds(a, size)], tok.at[kind, pl.ds(b, size)], to)]

    y_next, y_last = lax.rem(y + 1, NY), lax.rem(y + NY - 1, NY)

    def gather_first(m):
        return [
            send(ref.at[m], full.at[m, y], to)
            for to in (y_up, y_down)
            for ref, full in ((wi_ref, wi), (wo_ref, wo))
        ]

    def gather_second(m, first):
        arrive(first)
        copies = []
        for full, size in ((wi, QUARTER // 2), (wo, H // 2)):
            for place, half, to in ((y_last, 0, y_up), (y_next, 1, y_down)):
                part = full.at[m, place, pl.ds(half * size, size)]
                copies.append(send(part, part, to))
        return copies

    earlier = (
        lax.broadcasted_iota(jnp.int32, (FRAMES, FRAMES), 0)
        < lax.broadcasted_iota(jnp.int32, (FRAMES, FRAMES), 1)
    ).astype(BF16)
    place_row = lax.broadcasted_iota(jnp.int32, (PAIR, 2 * FRAMES), 0).astype(F32)
    members = [
        (z * PLANE + lax.rem(x + q // LOCAL, NX) * LOCAL + q % LOCAL).astype(F32)
        for q in range(PLANE)
    ]

    def routing(slot):
        ids, gates = rt[slot, pl.ds(0, 8), :], rt[slot, pl.ds(8, 8), :]
        gate = jnp.concatenate(
            [
                jnp.sum(jnp.where(ids == member, gates, 0.0), 0, keepdims=True)
                for member in members
            ],
            0,
        )
        named = jnp.where(gate > 0.0, 1.0, 0.0)
        place = jnp.dot(named.astype(BF16), earlier, preferred_element_type=F32)
        return gate, jnp.where(gate > 0.0, place, -100.0)

    inputs[0].wait()
    inputs[1].wait()
    rt[0, pl.ds(0, 8), :] = ids_held[...].astype(F32)
    own_gate, own_place = routing(0)
    own_match = [
        place_row[:EARLY, :FRAMES] == own_place[q : q + 1, :] for q in range(PLANE)
    ]
    own_hot = jnp.concatenate([jnp.where(match, 1.0, 0.0) for match in own_match], 0).astype(BF16)
    own_gate = jnp.concatenate(
        [
            jnp.sum(jnp.where(match, own_gate[q : q + 1, :], 0.0), 1, keepdims=True)
            for q, match in enumerate(own_match)
        ],
        0,
    )
    inputs[2].wait()
    inputs[3].wait()
    pl.semaphore_wait(barrier, len(peers))

    down_route, up_route = hop_route(0, 1), hop_route(0, -1)
    up, down = {}, {}
    for kind in range(2):
        down[kind] = hop(0, 1, kind)
        up[kind] = hop(0, -1, kind)
    first = [gather_first(0)]
    own = []
    for m in range(LOCAL):
        for k, (ref, full) in enumerate(((wi_ref, wi), (wo_ref, wo))):
            own.append(pltpu.make_async_copy(ref.at[m], full.at[m, y], own_sems.at[m, k]))
            own[-1].start()

    def prepare(p):
        gate_a, place_a = routing(2 * p)
        gate_b, place_b = routing(2 * p + 1)
        gate = jnp.concatenate([gate_a, gate_b], 1)
        place = jnp.concatenate([place_a, place_b + float(MOST)], 1)
        slot_gates = []
        for q in range(PLANE):
            match = place_row == place[q : q + 1, :]
            hot[p, q] = jnp.where(match, 1.0, 0.0).astype(BF16)
            slot_gates.append(
                jnp.sum(jnp.where(match, gate[q : q + 1, :], 0.0), 1, keepdims=True)
            )
        return jnp.concatenate(slot_gates, 0)

    def store(p, kind, rows, height, low, high, tile):
        for q in range(PLANE):
            d, m = q // LOCAL, q % LOCAL
            start = q * height + (low if height == PAIR else 0)
            block = rows[start : start + high - low]
            if d:
                xs[p, m, d - 1, kind, low:high, tile] = block
            else:
                xr[m, kind, pl.ds(p * NX * PAIR + low, high - low), tile] = block

    def pick(p, kind, slot_gate, low=0):
        source = pl.ds(p * 2 * FRAMES, 2 * FRAMES)
        chosen = hot[p].reshape(PLANE * PAIR, 2 * FRAMES)
        for start in range(0, D, TILE):
            tile = pl.ds(start, TILE)
            rows = jnp.dot(chosen, tok[kind, source, tile], preferred_element_type=F32)
            if kind:
                rows = rows * slot_gate
            store(p, kind, rows.astype(BF16), PAIR, low, PAIR, tile)

    rows_in = {(p, m): [] for p in range(PAIRS) for m in range(LOCAL)}

    def scatter(p, m, kind, low=0, high=PAIR):
        for d in range(1, NX):
            src = xs.at[p, m, d - 1, kind, pl.ds(low, high - low)]
            rows = pl.ds((p * NX + NX - d) * PAIR + low, high - low)
            rows_in[p, m].append(send(src, xr.at[m, kind, rows], x_far[d]))

    for kind in range(2):
        for start in range(0, D, TILE):
            tile = pl.ds(start, TILE)
            frames = tok[kind, pl.ds(0, FRAMES), tile]
            rows = jnp.dot(own_hot, frames, preferred_element_type=F32)
            if kind:
                rows = rows * own_gate
            store(0, kind, rows.astype(BF16), EARLY, 0, EARLY, tile)
        for m in range(LOCAL):
            scatter(0, m, kind, 0, EARLY)
    arrive(down_route)
    down_route = hop_route(1, 1)
    slot_gate = prepare(0)
    arrive(up_route)
    up_route = hop_route(7, -1)
    up_next, down_next = {}, {}
    for kind in range(2):
        arrive(down[kind])
        down_next[kind] = hop(1, 1, kind)
        arrive(up[kind])
        up_next[kind] = hop(7, -1, kind)
        pick(0, kind, slot_gate, EARLY)
        for m in range(LOCAL):
            scatter(0, m, kind, EARLY)
    up, down = up_next, down_next
    for p, (a, b) in ((1, (6, 2)), (2, (5, 3))):
        if p == 2:
            second = [gather_second(0, first[0])]
            first.append(gather_first(1))
        arrive(down_route)
        arrive(up_route)
        if p == 1:
            down_route = hop_route(b, 1)
        up_route = hop_route(a, -1)
        slot_gate = prepare(p)
        up_next, down_next = {}, {}
        for kind in range(2):
            arrive(down[kind])
            down_next[kind] = hop(b, 1, kind, 1 if p == 2 else None)
            arrive(up[kind])
            up_next[kind] = hop(a, -1, kind, 0 if p == 2 else None)
            pick(p, kind, slot_gate)
            scatter(p, 0, kind)
        up, down = up_next, down_next
    arrive(up_route)
    slot_gate = prepare(3)
    for kind in range(2):
        arrive(down[kind] + up[kind])
        pick(3, kind, slot_gate)
        scatter(3, 0, kind)
    for p in range(1, PAIRS):
        for kind in range(2):
            scatter(p, 1, kind)

    def forward(m, c):
        rows = pl.ds(c * CHUNK, CHUNK)

        @pl.loop(0, H // TILE)
        def _(n):
            columns = pl.ds(pl.multiple_of(n * TILE, TILE), TILE)
            pre = jnp.zeros((CHUNK, TILE), F32)
            hidden_grad = jnp.zeros((CHUNK, TILE), F32)
            for r in range(NY):
                part = pl.ds(r * QUARTER, QUARTER)
                pre += contract(xr[m, 0, rows, part], wi[m, r, :, columns], 1, 0)
                hidden_grad += contract(xr[m, 1, rows, part], wo[m, r, columns, :], 1, 1)
            sigma = jax.nn.sigmoid(pre)
            slope = sigma * (1.0 + pre * (1.0 - sigma))
            hb[columns, rows] = jnp.transpose(pre * sigma).astype(BF16)
            pb[rows, columns] = (hidden_grad * slope).astype(BF16)

    def backward(m, c):
        rows = pl.ds(c * CHUNK, CHUNK)

        @pl.loop(0, NY)
        def _(r):
            columns = pl.ds(pl.multiple_of(r * QUARTER, QUARTER), QUARTER)
            rg[m, rows, columns] = contract(pb[rows, :], wi[m, r], 1, 1).astype(BF16)

    def parts(m, j):
        columns = pl.ds(pl.multiple_of(lax.rem(y + j, NY) * QUARTER, QUARTER), QUARTER)
        pi[m, j] = contract(xr[m, 0, :, columns], pb[...], 0, 0).astype(BF16)
        po[m, j] = contract(hb[...], xr[m, 1, :, columns], 1, 0).astype(BF16)

    half_i, half_o = QUARTER // 2, H // 2

    def reduce_first(m):
        copies = []
        for way, to in ((0, y_up), (1, y_down)):
            copies.append(send(pi.at[m, 2, pl.ds(way * half_i, half_i)], hop_i.at[m, way], to))
            copies.append(send(po.at[m, 2, pl.ds(way * half_o, half_o)], hop_o.at[m, way], to))
        return copies

    def add(ref, place, term):
        ref[place] = (ref[place].astype(F32) + term.astype(F32)).astype(BF16)

    def reduce_second(m, copies):
        after = []
        for way, to in ((0, y_up), (1, y_down)):
            j = 1 if way == 0 else 3
            arrive(copies[2 * way : 2 * way + 2])
            add(pi, (m, j, pl.ds(way * half_i, half_i)), hop_i[m, way])
            add(po, (m, j, pl.ds(way * half_o, half_o)), hop_o[m, way])
            after.append(send(pi.at[m, j], end_i.at[m, way], to))
            after.append(send(po.at[m, j], end_o.at[m, way], to))
        return after

    outputs = []

    def reduce_last(m, copies):
        arrive(copies)
        for k, (out, part, end) in enumerate(((gi_ref, pi, end_i), (go_ref, po, end_o))):
            total = part[m, 0].astype(F32) + end[m, 0].astype(F32) + end[m, 1].astype(F32)
            part[m, 0] = total.astype(BF16)
            outputs.append(
                pltpu.make_async_copy(part.at[m, 0], out.at[m], local_sems.at[4 + 2 * m + k])
            )
            outputs[-1].start()

    back = {(p, low): [] for p in range(PAIRS) for low in (0, EARLY)}

    def rows_back(p, m, low=0, high=PAIR):
        for b in range(1, NX):
            rows = pl.ds((p * NX + b) * PAIR + low, high - low)
            place = rr.at[p, (NX - b) * LOCAL + m, pl.ds(low, high - low)]
            back[p, low].append(send(rg.at[m, rows], place, x_far[b]))
        rr[p, m, low:high, :] = rg[m, pl.ds(p * NX * PAIR + low, high - low), :]

    def combine(p, low, begin, end):
        chosen = hot[p, :, low:, begin:end].reshape(PLANE * (PAIR - low), end - begin)
        for start in range(0, D, TILE):
            tile = pl.ds(start, TILE)
            rows = rr[p, :, low:, tile].reshape(PLANE * (PAIR - low), TILE)
            total = contract(chosen, rows, 0, 0)
            par[pl.ds(p * 2 * FRAMES + begin, end - begin), tile] = total.astype(BF16)

    arrive(second[0])
    own[0].wait()
    own[1].wait()
    for c in range(2):
        for p in (2 * c, 2 * c + 1):
            arrive(rows_in[p, 0])
        forward(0, c)
    parts(0, 2)
    sums = [reduce_first(0)]
    second.append(gather_second(1, first[1]))
    parts(0, 1)
    parts(0, 3)
    parts(0, 0)
    for c in range(2):
        backward(0, c)
    sums[0] = reduce_second(0, sums[0])

    arrive(second[1])
    own[2].wait()
    own[3].wait()
    arrive(rows_in[0, 1] + rows_in[1, 1])
    forward(1, 0)
    backward(1, 0)
    arrive(rows_in[2, 1])
    rows_back(3, 0)
    arrive(rows_in[3, 1])
    rows_back(2, 0)
    forward(1, 1)
    parts(1, 2)
    sums.append(reduce_first(1))
    backward(1, 1)
    rows_back(3, 1)
    rows_back(2, 1)
    for p in (1, 0):
        for low, high in ((EARLY, PAIR), (0, EARLY)):
            for m in range(LOCAL):
                rows_back(p, m, low, high)
    parts(1, 1)
    parts(1, 3)
    parts(1, 0)
    reduce_last(0, sums[0])

    def chunk(distance, half=None):
        start, size = SLOT[distance] * FRAMES, FRAMES
        if half is not None:
            size = FRAMES // 2
            start += half * size
        return pl.ds(start, size)

    def returned(p):
        arrive(back[p, 0])
        combine(p, 0, 0, 2 * FRAMES)

    def returned_second(p):
        arrive(back[p, EARLY])
        combine(p, EARLY, FRAMES, 2 * FRAMES)

    def returned_first(p):
        arrive(back[p, 0])
        combine(p, 0, 0, FRAMES)

    returned(3)
    up = send(par.at[chunk(4, 0)], zhalf.at[0], z_up)
    down = send(par.at[chunk(4, 1)], zhalf.at[1], z_down)
    sums[1] = reduce_second(1, sums[1])
    returned(2)
    arrive([up])
    add(par, (chunk(3, 0),), zhalf[0])
    up = send(par.at[chunk(3)], zin.at[0, 0], z_up)
    arrive([down])
    add(par, (chunk(5, 1),), zhalf[1])
    down = send(par.at[chunk(5)], zin.at[1, 0], z_down)
    returned_second(1)
    arrive([up])
    add(par, (chunk(2),), zin[0, 0])
    up = send(par.at[chunk(2)], zin.at[0, 1], z_up)
    arrive([down])
    add(par, (chunk(6),), zin[1, 0])
    down = send(par.at[chunk(6)], zin.at[1, 1], z_down)
    returned_first(1)
    returned_second(0)
    arrive([up])
    add(par, (chunk(1),), zin[0, 1])
    up = send(par.at[chunk(1)], zin.at[0, 2], z_up_other)
    arrive([down])
    add(par, (chunk(7),), zin[1, 1])
    down = send(par.at[chunk(7)], zin.at[1, 2], z_down_other)
    returned_first(0)
    across = send(par.at[chunk(0)], fin, partner)
    reduce_last(1, sums[1])
    arrive([across, up, down])
    total = fin[...].astype(F32) + zin[0, 2].astype(F32) + zin[1, 2].astype(F32)
    sent_ref[...] = total.astype(BF16)
    for copy in outputs:
        copy.wait()
    for copy in started:
        copy.wait_send()


def publish(sent_in, gi_in, go_in, sent_out, gi_out, go_out, sent_held, gi_held, go_held, sems):
    trios = []
    for m in range(LOCAL):
        trios.append((gi_in.at[m], gi_held.at[m], gi_out.at[m]))
        trios.append((go_in.at[m], go_held.at[m], go_out.at[m]))
    trios.append((sent_in, sent_held, sent_out))
    inward = [pltpu.make_async_copy(a, h, sems.at[0, i]) for i, (a, h, _) in enumerate(trios)]
    outward = [pltpu.make_async_copy(h, b, sems.at[1, i]) for i, (_, h, b) in enumerate(trios)]
    for copy in inward:
        copy.start()
    for arriving, leaving in zip(inward, outward):
        arriving.wait()
        leaving.start()
    for copy in outward:
        copy.wait()


def per_device(frames, cotangent, expert_ids, gate_weights, weight_in, weight_out):
    vmem = pl.BlockSpec(memory_space=pltpu.VMEM)
    anywhere = pl.BlockSpec(memory_space=pl.ANY)
    shapes = (
        jax.ShapeDtypeStruct((FRAMES, D), BF16),
        jax.ShapeDtypeStruct((LOCAL, QUARTER, H), BF16),
        jax.ShapeDtypeStruct((LOCAL, H, QUARTER), BF16),
    )
    results = pl.pallas_call(
        kernel,
        name="relay",
        out_shape=shapes,
        in_specs=[anywhere] * 6,
        out_specs=(vmem, anywhere, anywhere),
        scratch_shapes=[
            pltpu.VMEM((2, NZ * FRAMES, D), BF16),
            pltpu.VMEM((NZ, 16, FRAMES), F32),
            pltpu.VMEM((PAIRS, PLANE, PAIR, 2 * FRAMES), BF16),
            pltpu.VMEM((PAIRS, LOCAL, NX - 1, 2, PAIR, D), BF16),
            pltpu.VMEM((LOCAL, 2, ROWS, D), BF16),
            pltpu.VMEM((LOCAL, NY, QUARTER, H), BF16),
            pltpu.VMEM((LOCAL, NY, H, QUARTER), BF16),
            pltpu.VMEM((H, ROWS), BF16),
            pltpu.VMEM((ROWS, H), BF16),
            pltpu.VMEM((LOCAL, ROWS, D), BF16),
            pltpu.VMEM((PAIRS, PLANE, PAIR, D), BF16),
            pltpu.VMEM((NZ * FRAMES, D), BF16),
            pltpu.VMEM((2, FRAMES // 2, D), BF16),
            pltpu.VMEM((2, 3, FRAMES, D), BF16),
            pltpu.VMEM((LOCAL, NY, QUARTER, H), BF16),
            pltpu.VMEM((LOCAL, NY, H, QUARTER), BF16),
            pltpu.VMEM((LOCAL, 2, QUARTER // 2, H), BF16),
            pltpu.VMEM((LOCAL, 2, H // 2, QUARTER), BF16),
            pltpu.VMEM((LOCAL, 2, QUARTER, H), BF16),
            pltpu.VMEM((LOCAL, 2, H, QUARTER), BF16),
            pltpu.VMEM((FRAMES, D), BF16),
            pltpu.VMEM((8, FRAMES), jnp.int32),
            pltpu.SemaphoreType.DMA((COPIES,)),
            pltpu.SemaphoreType.DMA((COPIES,)),
            pltpu.SemaphoreType.DMA((LOCAL, 2)),
            pltpu.SemaphoreType.DMA((4 + 2 * LOCAL,)),
        ],
        compiler_params=pltpu.CompilerParams(
            collective_id=0, has_side_effects=True, vmem_limit_bytes=60 * 2**20
        ),
    )(expert_ids[0].T, gate_weights[0].T, frames[0], cotangent[0], weight_in[0], weight_out[0])
    sent, grad_in, grad_out = pl.pallas_call(
        publish,
        name="publish",
        out_shape=shapes,
        in_specs=[anywhere] * 3,
        out_specs=(anywhere,) * 3,
        scratch_shapes=[
            *[pltpu.VMEM(shape.shape, shape.dtype) for shape in shapes],
            pltpu.SemaphoreType.DMA((2, 1 + 2 * LOCAL)),
        ],
    )(*results)
    return sent[None], grad_in[None], grad_out[None]


def solution(mesh):
    rows = P("section", ("expert", "replica"), None)
    first = P("section", "expert", "replica", None)
    second = P("section", "expert", None, "replica")
    return jax.shard_map(
        per_device,
        mesh=mesh,
        in_specs=(rows, rows, rows, rows, first, second),
        out_specs=(rows, first, second),
        check_vma=False,
    )
```

```python
import jax
import jax.numpy as jnp
from jax import lax
from jax.experimental import pallas as pl
from jax.experimental.pallas import tpu as pltpu
from jax.sharding import PartitionSpec as P

MESH = pl.DeviceIdType.MESH
NZ, NX, NY = 8, 4, 4
FRAMES = 128
D, H = 1024, 768
MOST = 24
PAIR = 2 * MOST
LOCAL = 2
PLANE = NX * LOCAL
ROWS = NZ * NX * MOST
CHUNK = ROWS // 2
QUARTER = D // NY
TILE = 256
COPIES = 176
EARLY = 16
ORDER = (0, 1, 7, 2, 6, 3, 5, 4)
SLOT = {distance: place for place, distance in enumerate(ORDER)}
PAIRS = len(ORDER) // 2
F32, BF16 = jnp.float32, jnp.bfloat16


def contract(a, b, dim_a, dim_b):
    return lax.dot_general(a, b, (((dim_a,), (dim_b,)), ((), ())), preferred_element_type=F32)


def kernel(
    ids_ref,
    gate_ref,
    x_ref,
    c_ref,
    wi_ref,
    wo_ref,
    sent_ref,
    gi_ref,
    go_ref,
    tok,
    rt,
    hot,
    xs,
    xr,
    wi,
    wo,
    hb,
    pb,
    rg,
    rr,
    par,
    zhalf,
    zin,
    pi,
    po,
    hop_i,
    hop_o,
    end_i,
    end_o,
    fin,
    ids_held,
    send_sems,
    recv_sems,
    own_sems,
    local_sems,
):
    expert = lax.axis_index("expert")
    z, x = expert // NX, expert % NX
    y, s = lax.axis_index("replica"), lax.axis_index("section")

    def device(dz, dx, dy):
        place = lax.rem(z + dz + NZ, NZ) * NX + lax.rem(x + dx + NX, NX)
        return place, lax.rem(y + dy + NY, NY), s

    z_up, z_down = device(1, 0, 0), device(-1, 0, 0)
    y_up, y_down = device(0, 0, 1), device(0, 0, -1)
    x_far = [device(0, d, 0) for d in range(NX)]
    partner = (expert, y, 1 - s)

    z_up_other, z_down_other = (*z_up[:2], 1 - s), (*z_down[:2], 1 - s)
    barrier = pltpu.get_barrier_semaphore()
    peers = [z_up, z_down, y_up, y_down, *x_far[1:], partner, z_up_other, z_down_other]
    for peer in peers:
        pl.semaphore_signal(barrier, inc=1, device_id=peer, device_id_type=MESH)
    inputs = [
        pltpu.make_async_copy(src, dst, local_sems.at[i])
        for i, (src, dst) in enumerate(
            (
                (ids_ref, ids_held),
                (gate_ref, rt.at[0, pl.ds(8, 8)]),
                (x_ref, tok.at[0, pl.ds(0, FRAMES)]),
                (c_ref, tok.at[1, pl.ds(0, FRAMES)]),
            )
        )
    ]
    for copy in inputs:
        copy.start()

    started = []

    def send(src, dst, to):
        number = len(started)
        copy = pltpu.make_async_remote_copy(
            src_ref=src,
            dst_ref=dst,
            send_sem=send_sems.at[number],
            recv_sem=recv_sems.at[number],
            device_id=to,
            device_id_type=MESH,
        )
        copy.start()
        started.append(copy)
        return copy

    def arrive(copies):
        for copy in copies:
            copy.wait_recv()

    def hop_route(distance, step):
        to = z_up if step < 0 else z_down
        return [send(rt.at[SLOT[distance]], rt.at[SLOT[(distance + step) % NZ]], to)]

    def hop(distance, step, kind, half=None):
        land = (distance + step) % NZ
        to = z_up if step < 0 else z_down
        a, b, size = SLOT[distance] * FRAMES, SLOT[land] * FRAMES, FRAMES
        if half is not None:
            size = FRAMES // 2
            a, b = a + half * size, b + half * size
        return [send(tok.at[kind, pl.ds(a, size)], tok.at[kind, pl.ds(b, size)], to)]

    y_next, y_last = lax.rem(y + 1, NY), lax.rem(y + NY - 1, NY)

    def gather_first(m):
        return [
            send(ref.at[m], full.at[m, y], to)
            for to in (y_up, y_down)
            for ref, full in ((wi_ref, wi), (wo_ref, wo))
        ]

    def gather_second(m, first):
        arrive(first)
        copies = []
        for full, size in ((wi, QUARTER // 2), (wo, H // 2)):
            for place, half, to in ((y_last, 0, y_up), (y_next, 1, y_down)):
                part = full.at[m, place, pl.ds(half * size, size)]
                copies.append(send(part, part, to))
        return copies

    earlier = (
        lax.broadcasted_iota(jnp.int32, (FRAMES, FRAMES), 0)
        < lax.broadcasted_iota(jnp.int32, (FRAMES, FRAMES), 1)
    ).astype(BF16)
    place_row = lax.broadcasted_iota(jnp.int32, (PAIR, 2 * FRAMES), 0).astype(F32)
    members = [
        (z * PLANE + lax.rem(x + q // LOCAL, NX) * LOCAL + q % LOCAL).astype(F32)
        for q in range(PLANE)
    ]

    def routing(slot):
        ids, gates = rt[slot, pl.ds(0, 8), :], rt[slot, pl.ds(8, 8), :]
        gate = jnp.concatenate(
            [
                jnp.sum(jnp.where(ids == member, gates, 0.0), 0, keepdims=True)
                for member in members
            ],
            0,
        )
        named = jnp.where(gate > 0.0, 1.0, 0.0)
        place = jnp.dot(named.astype(BF16), earlier, preferred_element_type=F32)
        return gate, jnp.where(gate > 0.0, place, -100.0)

    inputs[0].wait()
    inputs[1].wait()
    rt[0, pl.ds(0, 8), :] = ids_held[...].astype(F32)
    own_gate, own_place = routing(0)
    own_match = [
        place_row[:EARLY, :FRAMES] == own_place[q : q + 1, :] for q in range(PLANE)
    ]
    own_hot = jnp.concatenate([jnp.where(match, 1.0, 0.0) for match in own_match], 0).astype(BF16)
    own_gate = jnp.concatenate(
        [
            jnp.sum(jnp.where(match, own_gate[q : q + 1, :], 0.0), 1, keepdims=True)
            for q, match in enumerate(own_match)
        ],
        0,
    )
    inputs[2].wait()
    inputs[3].wait()
    pl.semaphore_wait(barrier, len(peers))

    down_route, up_route = hop_route(0, 1), hop_route(0, -1)
    up, down = {}, {}
    for kind in range(2):
        down[kind] = hop(0, 1, kind)
        up[kind] = hop(0, -1, kind)
    first = [gather_first(0)]
    own = []
    for m in range(LOCAL):
        for k, (ref, full) in enumerate(((wi_ref, wi), (wo_ref, wo))):
            own.append(pltpu.make_async_copy(ref.at[m], full.at[m, y], own_sems.at[m, k]))
            own[-1].start()

    def prepare(p):
        gate_a, place_a = routing(2 * p)
        gate_b, place_b = routing(2 * p + 1)
        gate = jnp.concatenate([gate_a, gate_b], 1)
        place = jnp.concatenate([place_a, place_b + float(MOST)], 1)
        slot_gates = []
        for q in range(PLANE):
            match = place_row == place[q : q + 1, :]
            hot[p, q] = jnp.where(match, 1.0, 0.0).astype(BF16)
            slot_gates.append(
                jnp.sum(jnp.where(match, gate[q : q + 1, :], 0.0), 1, keepdims=True)
            )
        return jnp.concatenate(slot_gates, 0)

    def store(p, kind, rows, height, low, high, tile):
        for q in range(PLANE):
            d, m = q // LOCAL, q % LOCAL
            start = q * height + (low if height == PAIR else 0)
            block = rows[start : start + high - low]
            if d:
                xs[p, m, d - 1, kind, low:high, tile] = block
            else:
                xr[m, kind, pl.ds(p * NX * PAIR + low, high - low), tile] = block

    def pick(p, kind, slot_gate, low=0):
        source = pl.ds(p * 2 * FRAMES, 2 * FRAMES)
        chosen = hot[p].reshape(PLANE * PAIR, 2 * FRAMES)
        for start in range(0, D, TILE):
            tile = pl.ds(start, TILE)
            rows = jnp.dot(chosen, tok[kind, source, tile], preferred_element_type=F32)
            if kind:
                rows = rows * slot_gate
            store(p, kind, rows.astype(BF16), PAIR, low, PAIR, tile)

    rows_in = {(p, m): [] for p in range(PAIRS) for m in range(LOCAL)}

    def scatter(p, m, kind, low=0, high=PAIR):
        for d in range(1, NX):
            src = xs.at[p, m, d - 1, kind, pl.ds(low, high - low)]
            rows = pl.ds((p * NX + NX - d) * PAIR + low, high - low)
            rows_in[p, m].append(send(src, xr.at[m, kind, rows], x_far[d]))

    for kind in range(2):
        for start in range(0, D, TILE):
            tile = pl.ds(start, TILE)
            frames = tok[kind, pl.ds(0, FRAMES), tile]
            rows = jnp.dot(own_hot, frames, preferred_element_type=F32)
            if kind:
                rows = rows * own_gate
            store(0, kind, rows.astype(BF16), EARLY, 0, EARLY, tile)
        for m in range(LOCAL):
            scatter(0, m, kind, 0, EARLY)
    arrive(down_route)
    down_route = hop_route(1, 1)
    slot_gate = prepare(0)
    arrive(up_route)
    up_route = hop_route(7, -1)
    up_next, down_next = {}, {}
    for kind in range(2):
        arrive(down[kind])
        down_next[kind] = hop(1, 1, kind)
        arrive(up[kind])
        up_next[kind] = hop(7, -1, kind)
        pick(0, kind, slot_gate, EARLY)
        for m in range(LOCAL):
            scatter(0, m, kind, EARLY)
    up, down = up_next, down_next
    for p, (a, b) in ((1, (6, 2)), (2, (5, 3))):
        arrive(down_route)
        arrive(up_route)
        if p == 1:
            down_route = hop_route(b, 1)
        up_route = hop_route(a, -1)
        slot_gate = prepare(p)
        up_next, down_next = {}, {}
        for kind in range(2):
            arrive(down[kind])
            down_next[kind] = hop(b, 1, kind, 1 if p == 2 else None)
            arrive(up[kind])
            up_next[kind] = hop(a, -1, kind, 0 if p == 2 else None)
            pick(p, kind, slot_gate)
            scatter(p, 0, kind)
            if p == 1:
                scatter(p, 1, kind)
                if kind == 0:
                    second = [gather_second(0, first[0])]
                    first.append(gather_first(1))
        up, down = up_next, down_next
    arrive(up_route)
    slot_gate = prepare(3)
    for kind in range(2):
        arrive(down[kind] + up[kind])
        pick(3, kind, slot_gate)
        scatter(3, 0, kind)
    for p in (2, 3):
        for kind in range(2):
            scatter(p, 1, kind)

    def forward(m, c):
        rows = pl.ds(c * CHUNK, CHUNK)

        @pl.loop(0, H // TILE)
        def _(n):
            columns = pl.ds(pl.multiple_of(n * TILE, TILE), TILE)
            pre = jnp.zeros((CHUNK, TILE), F32)
            hidden_grad = jnp.zeros((CHUNK, TILE), F32)
            for r in range(NY):
                part = pl.ds(r * QUARTER, QUARTER)
                pre += contract(xr[m, 0, rows, part], wi[m, r, :, columns], 1, 0)
                hidden_grad += contract(xr[m, 1, rows, part], wo[m, r, columns, :], 1, 1)
            sigma = jax.nn.sigmoid(pre)
            slope = sigma * (1.0 + pre * (1.0 - sigma))
            hb[columns, rows] = jnp.transpose(pre * sigma).astype(BF16)
            pb[rows, columns] = (hidden_grad * slope).astype(BF16)

    def backward(m, c):
        rows = pl.ds(c * CHUNK, CHUNK)

        @pl.loop(0, NY)
        def _(r):
            columns = pl.ds(pl.multiple_of(r * QUARTER, QUARTER), QUARTER)
            rg[m, rows, columns] = contract(pb[rows, :], wi[m, r], 1, 1).astype(BF16)

    def parts(m, j):
        columns = pl.ds(pl.multiple_of(lax.rem(y + j, NY) * QUARTER, QUARTER), QUARTER)
        pi[m, j] = contract(xr[m, 0, :, columns], pb[...], 0, 0).astype(BF16)
        po[m, j] = contract(hb[...], xr[m, 1, :, columns], 1, 0).astype(BF16)

    half_i, half_o = QUARTER // 2, H // 2

    def reduce_first(m):
        copies = []
        for way, to in ((0, y_up), (1, y_down)):
            copies.append(send(pi.at[m, 2, pl.ds(way * half_i, half_i)], hop_i.at[m, way], to))
            copies.append(send(po.at[m, 2, pl.ds(way * half_o, half_o)], hop_o.at[m, way], to))
        return copies

    def add(ref, place, term):
        ref[place] = (ref[place].astype(F32) + term.astype(F32)).astype(BF16)

    def reduce_second(m, copies):
        after = []
        for way, to in ((0, y_up), (1, y_down)):
            j = 1 if way == 0 else 3
            arrive(copies[2 * way : 2 * way + 2])
            add(pi, (m, j, pl.ds(way * half_i, half_i)), hop_i[m, way])
            add(po, (m, j, pl.ds(way * half_o, half_o)), hop_o[m, way])
            after.append(send(pi.at[m, j], end_i.at[m, way], to))
            after.append(send(po.at[m, j], end_o.at[m, way], to))
        return after

    outputs = []

    def reduce_last(m, copies):
        arrive(copies)
        for k, (out, part, end) in enumerate(((gi_ref, pi, end_i), (go_ref, po, end_o))):
            total = part[m, 0].astype(F32) + end[m, 0].astype(F32) + end[m, 1].astype(F32)
            part[m, 0] = total.astype(BF16)
            outputs.append(
                pltpu.make_async_copy(part.at[m, 0], out.at[m], local_sems.at[4 + 2 * m + k])
            )
            outputs[-1].start()

    back = {(p, low): [] for p in range(PAIRS) for low in (0, EARLY)}

    def rows_back(p, m, low=0, high=PAIR):
        for b in range(1, NX):
            rows = pl.ds((p * NX + b) * PAIR + low, high - low)
            place = rr.at[p, (NX - b) * LOCAL + m, pl.ds(low, high - low)]
            back[p, low].append(send(rg.at[m, rows], place, x_far[b]))
        rr[p, m, low:high, :] = rg[m, pl.ds(p * NX * PAIR + low, high - low), :]

    def combine(p, low, begin, end):
        chosen = hot[p, :, low:, begin:end].reshape(PLANE * (PAIR - low), end - begin)
        for start in range(0, D, TILE):
            tile = pl.ds(start, TILE)
            rows = rr[p, :, low:, tile].reshape(PLANE * (PAIR - low), TILE)
            total = contract(chosen, rows, 0, 0)
            par[pl.ds(p * 2 * FRAMES + begin, end - begin), tile] = total.astype(BF16)

    arrive(second[0])
    own[0].wait()
    own[1].wait()
    for c in range(2):
        for p in (2 * c, 2 * c + 1):
            arrive(rows_in[p, 0])
        forward(0, c)
        if c == 0:
            second.append(gather_second(1, first[1]))
    parts(0, 2)
    sums = [reduce_first(0)]
    parts(0, 1)
    parts(0, 3)
    parts(0, 0)
    for c in range(2):
        backward(0, c)

    arrive(second[1])
    own[2].wait()
    own[3].wait()
    arrive(rows_in[0, 1] + rows_in[1, 1])
    forward(1, 0)
    backward(1, 0)
    sums[0] = reduce_second(0, sums[0])
    arrive(rows_in[2, 1])
    rows_back(3, 0)
    arrive(rows_in[3, 1])
    rows_back(2, 0)
    forward(1, 1)
    parts(1, 2)
    sums.append(reduce_first(1))
    backward(1, 1)
    rows_back(3, 1)
    rows_back(2, 1)
    for p in (1, 0):
        for low, high in ((EARLY, PAIR), (0, EARLY)):
            for m in range(LOCAL):
                rows_back(p, m, low, high)
    parts(1, 1)
    parts(1, 3)
    parts(1, 0)
    reduce_last(0, sums[0])

    def chunk(distance, half=None):
        start, size = SLOT[distance] * FRAMES, FRAMES
        if half is not None:
            size = FRAMES // 2
            start += half * size
        return pl.ds(start, size)

    def returned(p):
        arrive(back[p, 0])
        combine(p, 0, 0, 2 * FRAMES)

    def returned_second(p):
        arrive(back[p, EARLY])
        combine(p, EARLY, FRAMES, 2 * FRAMES)

    def returned_first(p):
        arrive(back[p, 0])
        combine(p, 0, 0, FRAMES)

    returned(3)
    up = send(par.at[chunk(4, 0)], zhalf.at[0], z_up)
    down = send(par.at[chunk(4, 1)], zhalf.at[1], z_down)
    sums[1] = reduce_second(1, sums[1])
    returned(2)
    arrive([up])
    add(par, (chunk(3, 0),), zhalf[0])
    up = send(par.at[chunk(3)], zin.at[0, 0], z_up)
    arrive([down])
    add(par, (chunk(5, 1),), zhalf[1])
    down = send(par.at[chunk(5)], zin.at[1, 0], z_down)
    returned_second(1)
    arrive([up])
    add(par, (chunk(2),), zin[0, 0])
    up = send(par.at[chunk(2)], zin.at[0, 1], z_up)
    arrive([down])
    add(par, (chunk(6),), zin[1, 0])
    down = send(par.at[chunk(6)], zin.at[1, 1], z_down)
    returned_first(1)
    returned_second(0)
    arrive([up])
    add(par, (chunk(1),), zin[0, 1])
    up = send(par.at[chunk(1)], zin.at[0, 2], z_up_other)
    arrive([down])
    add(par, (chunk(7),), zin[1, 1])
    down = send(par.at[chunk(7)], zin.at[1, 2], z_down_other)
    returned_first(0)
    across = send(par.at[chunk(0)], fin, partner)
    reduce_last(1, sums[1])
    late = (across, up, down)
    for copy in started:
        if all(copy is not other for other in late):
            copy.wait_send()
    arrive(late)
    total = fin[...].astype(F32) + zin[0, 2].astype(F32) + zin[1, 2].astype(F32)
    sent_ref[...] = total.astype(BF16)
    for copy in outputs:
        copy.wait()
    for copy in late:
        copy.wait_send()


def publish(sent_in, gi_in, go_in, sent_out, gi_out, go_out, sent_held, gi_held, go_held, sems):
    trios = []
    for m in range(LOCAL):
        trios.append((gi_in.at[m], gi_held.at[m], gi_out.at[m]))
        trios.append((go_in.at[m], go_held.at[m], go_out.at[m]))
    trios.append((sent_in, sent_held, sent_out))
    inward = [pltpu.make_async_copy(a, h, sems.at[0, i]) for i, (a, h, _) in enumerate(trios)]
    outward = [pltpu.make_async_copy(h, b, sems.at[1, i]) for i, (_, h, b) in enumerate(trios)]
    for copy in inward:
        copy.start()
    for arriving, leaving in zip(inward, outward):
        arriving.wait()
        leaving.start()
    for copy in outward:
        copy.wait()


def per_device(frames, cotangent, expert_ids, gate_weights, weight_in, weight_out):
    vmem = pl.BlockSpec(memory_space=pltpu.VMEM)
    anywhere = pl.BlockSpec(memory_space=pl.ANY)
    shapes = (
        jax.ShapeDtypeStruct((FRAMES, D), BF16),
        jax.ShapeDtypeStruct((LOCAL, QUARTER, H), BF16),
        jax.ShapeDtypeStruct((LOCAL, H, QUARTER), BF16),
    )
    results = pl.pallas_call(
        kernel,
        name="relay",
        out_shape=shapes,
        in_specs=[anywhere] * 6,
        out_specs=(vmem, anywhere, anywhere),
        scratch_shapes=[
            pltpu.VMEM((2, NZ * FRAMES, D), BF16),
            pltpu.VMEM((NZ, 16, FRAMES), F32),
            pltpu.VMEM((PAIRS, PLANE, PAIR, 2 * FRAMES), BF16),
            pltpu.VMEM((PAIRS, LOCAL, NX - 1, 2, PAIR, D), BF16),
            pltpu.VMEM((LOCAL, 2, ROWS, D), BF16),
            pltpu.VMEM((LOCAL, NY, QUARTER, H), BF16),
            pltpu.VMEM((LOCAL, NY, H, QUARTER), BF16),
            pltpu.VMEM((H, ROWS), BF16),
            pltpu.VMEM((ROWS, H), BF16),
            pltpu.VMEM((LOCAL, ROWS, D), BF16),
            pltpu.VMEM((PAIRS, PLANE, PAIR, D), BF16),
            pltpu.VMEM((NZ * FRAMES, D), BF16),
            pltpu.VMEM((2, FRAMES // 2, D), BF16),
            pltpu.VMEM((2, 3, FRAMES, D), BF16),
            pltpu.VMEM((LOCAL, NY, QUARTER, H), BF16),
            pltpu.VMEM((LOCAL, NY, H, QUARTER), BF16),
            pltpu.VMEM((LOCAL, 2, QUARTER // 2, H), BF16),
            pltpu.VMEM((LOCAL, 2, H // 2, QUARTER), BF16),
            pltpu.VMEM((LOCAL, 2, QUARTER, H), BF16),
            pltpu.VMEM((LOCAL, 2, H, QUARTER), BF16),
            pltpu.VMEM((FRAMES, D), BF16),
            pltpu.VMEM((8, FRAMES), jnp.int32),
            pltpu.SemaphoreType.DMA((COPIES,)),
            pltpu.SemaphoreType.DMA((COPIES,)),
            pltpu.SemaphoreType.DMA((LOCAL, 2)),
            pltpu.SemaphoreType.DMA((4 + 2 * LOCAL,)),
        ],
        compiler_params=pltpu.CompilerParams(
            collective_id=0, has_side_effects=True, vmem_limit_bytes=60 * 2**20
        ),
    )(expert_ids[0].T, gate_weights[0].T, frames[0], cotangent[0], weight_in[0], weight_out[0])
    sent, grad_in, grad_out = pl.pallas_call(
        publish,
        name="publish",
        out_shape=shapes,
        in_specs=[anywhere] * 3,
        out_specs=(anywhere,) * 3,
        scratch_shapes=[
            *[pltpu.VMEM(shape.shape, shape.dtype) for shape in shapes],
            pltpu.SemaphoreType.DMA((2, 1 + 2 * LOCAL)),
        ],
    )(*results)
    return sent[None], grad_in[None], grad_out[None]


def solution(mesh):
    rows = P("section", ("expert", "replica"), None)
    first = P("section", "expert", "replica", None)
    second = P("section", "expert", None, "replica")
    return jax.shard_map(
        per_device,
        mesh=mesh,
        in_specs=(rows, rows, rows, rows, first, second),
        out_specs=(rows, first, second),
        check_vma=False,
    )
```

```python
import jax
import jax.numpy as jnp
from jax import lax
from jax.experimental import pallas as pl
from jax.experimental.pallas import tpu as pltpu
from jax.sharding import PartitionSpec as P

MESH = pl.DeviceIdType.MESH
NZ, NX, NY = 8, 4, 4
FRAMES = 128
D, H = 1024, 768
MOST = 24
PAIR = 2 * MOST
LOCAL = 2
PLANE = NX * LOCAL
ROWS = NZ * NX * MOST
CHUNK = ROWS // 2
QUARTER = D // NY
TILE = 256
COPIES = 192
HALVES = ((0, D // 2), (D // 2, D // 2))
EARLY = 16
ORDER = (0, 1, 7, 2, 6, 3, 5, 4)
SLOT = {distance: place for place, distance in enumerate(ORDER)}
PAIRS = len(ORDER) // 2
F32, BF16 = jnp.float32, jnp.bfloat16


def contract(a, b, dim_a, dim_b):
    return lax.dot_general(a, b, (((dim_a,), (dim_b,)), ((), ())), preferred_element_type=F32)


def kernel(
    ids_ref,
    gate_ref,
    x_ref,
    c_ref,
    wi_ref,
    wo_ref,
    sent_ref,
    gi_ref,
    go_ref,
    tok,
    rt,
    hot,
    xs,
    xr,
    wi,
    wo,
    hb,
    pb,
    rg,
    rr,
    par,
    zhalf,
    zin,
    pi,
    po,
    hop_i,
    hop_o,
    end_i,
    end_o,
    fin,
    ids_held,
    send_sems,
    recv_sems,
    own_sems,
    local_sems,
):
    expert = lax.axis_index("expert")
    z, x = expert // NX, expert % NX
    y, s = lax.axis_index("replica"), lax.axis_index("section")

    def device(dz, dx, dy):
        place = lax.rem(z + dz + NZ, NZ) * NX + lax.rem(x + dx + NX, NX)
        return place, lax.rem(y + dy + NY, NY), s

    z_up, z_down = device(1, 0, 0), device(-1, 0, 0)
    y_up, y_down = device(0, 0, 1), device(0, 0, -1)
    x_far = [device(0, d, 0) for d in range(NX)]
    partner = (expert, y, 1 - s)

    z_up_other, z_down_other = (*z_up[:2], 1 - s), (*z_down[:2], 1 - s)
    barrier = pltpu.get_barrier_semaphore()
    peers = [z_up, z_down, y_up, y_down, *x_far[1:], partner, z_up_other, z_down_other]
    for peer in peers:
        pl.semaphore_signal(barrier, inc=1, device_id=peer, device_id_type=MESH)
    inputs = [
        pltpu.make_async_copy(src, dst, local_sems.at[i])
        for i, (src, dst) in enumerate(
            (
                (ids_ref, ids_held),
                (gate_ref, rt.at[0, pl.ds(8, 8)]),
                (x_ref, tok.at[0, pl.ds(0, FRAMES)]),
                (c_ref, tok.at[1, pl.ds(0, FRAMES)]),
            )
        )
    ]
    for copy in inputs:
        copy.start()

    started = []

    def send(src, dst, to):
        number = len(started)
        copy = pltpu.make_async_remote_copy(
            src_ref=src,
            dst_ref=dst,
            send_sem=send_sems.at[number],
            recv_sem=recv_sems.at[number],
            device_id=to,
            device_id_type=MESH,
        )
        copy.start()
        started.append(copy)
        return copy

    def arrive(copies):
        for copy in copies:
            copy.wait_recv()

    def hop_route(distance, step):
        to = z_up if step < 0 else z_down
        return [send(rt.at[SLOT[distance]], rt.at[SLOT[(distance + step) % NZ]], to)]

    def hop(distance, step, kind, half=None):
        land = (distance + step) % NZ
        to = z_up if step < 0 else z_down
        a, b, size = SLOT[distance] * FRAMES, SLOT[land] * FRAMES, FRAMES
        if half is not None:
            size = FRAMES // 2
            a, b = a + half * size, b + half * size
        return [send(tok.at[kind, pl.ds(a, size)], tok.at[kind, pl.ds(b, size)], to)]

    y_next, y_last = lax.rem(y + 1, NY), lax.rem(y + NY - 1, NY)

    def gather_first(m):
        return [
            send(ref.at[m], full.at[m, y], to)
            for to in (y_up, y_down)
            for ref, full in ((wi_ref, wi), (wo_ref, wo))
        ]

    def gather_second(m, first):
        arrive(first)
        copies = []
        for full, size in ((wi, QUARTER // 2), (wo, H // 2)):
            for place, half, to in ((y_last, 0, y_up), (y_next, 1, y_down)):
                part = full.at[m, place, pl.ds(half * size, size)]
                copies.append(send(part, part, to))
        return copies

    earlier = (
        lax.broadcasted_iota(jnp.int32, (FRAMES, FRAMES), 0)
        < lax.broadcasted_iota(jnp.int32, (FRAMES, FRAMES), 1)
    ).astype(BF16)
    place_row = lax.broadcasted_iota(jnp.int32, (PAIR, 2 * FRAMES), 0).astype(F32)
    members = [
        (z * PLANE + lax.rem(x + q // LOCAL, NX) * LOCAL + q % LOCAL).astype(F32)
        for q in range(PLANE)
    ]

    def routing(slot):
        ids, gates = rt[slot, pl.ds(0, 8), :], rt[slot, pl.ds(8, 8), :]
        gate = jnp.concatenate(
            [
                jnp.sum(jnp.where(ids == member, gates, 0.0), 0, keepdims=True)
                for member in members
            ],
            0,
        )
        named = jnp.where(gate > 0.0, 1.0, 0.0)
        place = jnp.dot(named.astype(BF16), earlier, preferred_element_type=F32)
        return gate, jnp.where(gate > 0.0, place, -100.0)

    inputs[0].wait()
    inputs[1].wait()
    rt[0, pl.ds(0, 8), :] = ids_held[...].astype(F32)
    own_gate, own_place = routing(0)
    own_match = [
        place_row[:EARLY, :FRAMES] == own_place[q : q + 1, :] for q in range(PLANE)
    ]
    own_hot = jnp.concatenate([jnp.where(match, 1.0, 0.0) for match in own_match], 0).astype(BF16)
    own_gate = jnp.concatenate(
        [
            jnp.sum(jnp.where(match, own_gate[q : q + 1, :], 0.0), 1, keepdims=True)
            for q, match in enumerate(own_match)
        ],
        0,
    )
    inputs[2].wait()
    inputs[3].wait()
    pl.semaphore_wait(barrier, len(peers))

    down_route, up_route = hop_route(0, 1), hop_route(0, -1)
    up, down = {}, {}
    for kind in range(2):
        down[kind] = hop(0, 1, kind)
        up[kind] = hop(0, -1, kind)
    first = [gather_first(0)]
    own = []
    for m in range(LOCAL):
        for k, (ref, full) in enumerate(((wi_ref, wi), (wo_ref, wo))):
            own.append(pltpu.make_async_copy(ref.at[m], full.at[m, y], own_sems.at[m, k]))
            own[-1].start()

    def prepare(p):
        gate_a, place_a = routing(2 * p)
        gate_b, place_b = routing(2 * p + 1)
        gate = jnp.concatenate([gate_a, gate_b], 1)
        place = jnp.concatenate([place_a, place_b + float(MOST)], 1)
        slot_gates = []
        for q in range(PLANE):
            match = place_row == place[q : q + 1, :]
            hot[p, q] = jnp.where(match, 1.0, 0.0).astype(BF16)
            slot_gates.append(
                jnp.sum(jnp.where(match, gate[q : q + 1, :], 0.0), 1, keepdims=True)
            )
        return jnp.concatenate(slot_gates, 0)

    def store(p, kind, rows, height, low, high, tile):
        for q in range(PLANE):
            d, m = q // LOCAL, q % LOCAL
            start = q * height + (low if height == PAIR else 0)
            block = rows[start : start + high - low]
            if d:
                xs[p, m, d - 1, kind, low:high, tile] = block
            else:
                xr[m, kind, pl.ds(p * NX * PAIR + low, high - low), tile] = block

    def pick(p, kind, slot_gate, low=0):
        source = pl.ds(p * 2 * FRAMES, 2 * FRAMES)
        chosen = hot[p].reshape(PLANE * PAIR, 2 * FRAMES)
        for start in range(0, D, TILE):
            tile = pl.ds(start, TILE)
            rows = jnp.dot(chosen, tok[kind, source, tile], preferred_element_type=F32)
            if kind:
                rows = rows * slot_gate
            store(p, kind, rows.astype(BF16), PAIR, low, PAIR, tile)

    rows_in = {(p, m): [] for p in range(PAIRS) for m in range(LOCAL)}

    def scatter(p, m, kind, low=0, high=PAIR):
        for d in range(1, NX):
            src = xs.at[p, m, d - 1, kind, pl.ds(low, high - low)]
            rows = pl.ds((p * NX + NX - d) * PAIR + low, high - low)
            rows_in[p, m].append(send(src, xr.at[m, kind, rows], x_far[d]))

    for kind in range(2):
        for start in range(0, D, TILE):
            tile = pl.ds(start, TILE)
            frames = tok[kind, pl.ds(0, FRAMES), tile]
            rows = jnp.dot(own_hot, frames, preferred_element_type=F32)
            if kind:
                rows = rows * own_gate
            store(0, kind, rows.astype(BF16), EARLY, 0, EARLY, tile)
        for m in range(LOCAL):
            scatter(0, m, kind, 0, EARLY)
    arrive(down_route)
    down_route = hop_route(1, 1)
    slot_gate = prepare(0)
    arrive(up_route)
    up_route = hop_route(7, -1)
    up_next, down_next = {}, {}
    for kind in range(2):
        arrive(down[kind])
        down_next[kind] = hop(1, 1, kind)
        arrive(up[kind])
        up_next[kind] = hop(7, -1, kind)
        pick(0, kind, slot_gate, EARLY)
        for m in range(LOCAL):
            scatter(0, m, kind, EARLY)
    up, down = up_next, down_next
    for p, (a, b) in ((1, (6, 2)), (2, (5, 3))):
        arrive(down_route)
        arrive(up_route)
        if p == 1:
            down_route = hop_route(b, 1)
        up_route = hop_route(a, -1)
        slot_gate = prepare(p)
        up_next, down_next = {}, {}
        for kind in range(2):
            arrive(down[kind])
            down_next[kind] = hop(b, 1, kind, 1 if p == 2 else None)
            arrive(up[kind])
            up_next[kind] = hop(a, -1, kind, 0 if p == 2 else None)
            pick(p, kind, slot_gate)
            scatter(p, 0, kind)
            if p == 1:
                scatter(p, 1, kind)
                if kind == 0:
                    second = [gather_second(0, first[0])]
                    first.append(gather_first(1))
        up, down = up_next, down_next
    arrive(up_route)
    slot_gate = prepare(3)
    for kind in range(2):
        arrive(down[kind] + up[kind])
        pick(3, kind, slot_gate)
        scatter(3, 0, kind)
    for p in (2, 3):
        for kind in range(2):
            scatter(p, 1, kind)

    def forward(m, c):
        rows = pl.ds(c * CHUNK, CHUNK)

        @pl.loop(0, H // TILE)
        def _(n):
            columns = pl.ds(pl.multiple_of(n * TILE, TILE), TILE)
            pre = jnp.zeros((CHUNK, TILE), F32)
            hidden_grad = jnp.zeros((CHUNK, TILE), F32)
            for r in range(NY):
                part = pl.ds(r * QUARTER, QUARTER)
                pre += contract(xr[m, 0, rows, part], wi[m, r, :, columns], 1, 0)
                hidden_grad += contract(xr[m, 1, rows, part], wo[m, r, columns, :], 1, 1)
            sigma = jax.nn.sigmoid(pre)
            slope = sigma * (1.0 + pre * (1.0 - sigma))
            hb[columns, rows] = jnp.transpose(pre * sigma).astype(BF16)
            pb[rows, columns] = (hidden_grad * slope).astype(BF16)

    def backward(m, c):
        rows = pl.ds(c * CHUNK, CHUNK)

        @pl.loop(0, NY)
        def _(r):
            columns = pl.ds(pl.multiple_of(r * QUARTER, QUARTER), QUARTER)
            rg[m, rows, columns] = contract(pb[rows, :], wi[m, r], 1, 1).astype(BF16)

    def parts(m, j):
        columns = pl.ds(pl.multiple_of(lax.rem(y + j, NY) * QUARTER, QUARTER), QUARTER)
        pi[m, j] = contract(xr[m, 0, :, columns], pb[...], 0, 0).astype(BF16)
        po[m, j] = contract(hb[...], xr[m, 1, :, columns], 1, 0).astype(BF16)

    half_i, half_o = QUARTER // 2, H // 2

    def reduce_first(m):
        copies = []
        for way, to in ((0, y_up), (1, y_down)):
            copies.append(send(pi.at[m, 2, pl.ds(way * half_i, half_i)], hop_i.at[m, way], to))
            copies.append(send(po.at[m, 2, pl.ds(way * half_o, half_o)], hop_o.at[m, way], to))
        return copies

    def add(ref, place, term):
        ref[place] = (ref[place].astype(F32) + term.astype(F32)).astype(BF16)

    ends = {(m, way): [] for m in range(LOCAL) for way in range(2)}

    def reduce_to(m, way, half, to):
        j = 1 if way == 0 else 3
        for part, end, size in ((pi, end_i, half_i), (po, end_o, half_o)):
            rows = pl.ds(half * size, size)
            ends[m, way].append(send(part.at[m, j, rows], end.at[m, way, rows], to))

    def reduce_alone(m):
        for way, to in ((0, y_up), (1, y_down)):
            reduce_to(m, way, 1 - way, to)

    def reduce_second(m, copies):
        for way, to in ((0, y_up), (1, y_down)):
            j = 1 if way == 0 else 3
            arrive(copies[2 * way : 2 * way + 2])
            add(pi, (m, j, pl.ds(way * half_i, half_i)), hop_i[m, way])
            add(po, (m, j, pl.ds(way * half_o, half_o)), hop_o[m, way])
            reduce_to(m, way, way, to)
        return ends[m, 0] + ends[m, 1]

    outputs = []

    def reduce_last(m, copies):
        arrive(copies)
        for k, (out, part, end) in enumerate(((gi_ref, pi, end_i), (go_ref, po, end_o))):
            total = part[m, 0].astype(F32) + end[m, 0].astype(F32) + end[m, 1].astype(F32)
            part[m, 0] = total.astype(BF16)
            outputs.append(
                pltpu.make_async_copy(part.at[m, 0], out.at[m], local_sems.at[4 + 2 * m + k])
            )
            outputs[-1].start()

    back = {}

    def rows_back(p, m, low=0, high=PAIR, columns=(0, D)):
        part = pl.ds(*columns)
        for b in range(1, NX):
            rows = pl.ds((p * NX + b) * PAIR + low, high - low)
            place = rr.at[p, (NX - b) * LOCAL + m, pl.ds(low, high - low), part]
            copy = send(rg.at[m, rows, part], place, x_far[b])
            back.setdefault((p, low, columns), []).append(copy)
        rr[p, m, low:high, part] = rg[m, pl.ds(p * NX * PAIR + low, high - low), part]

    def combine(p, low, begin, end, columns=(0, D)):
        chosen = hot[p, :, low:, begin:end].reshape(PLANE * (PAIR - low), end - begin)
        for start in range(columns[0], columns[0] + columns[1], TILE):
            tile = pl.ds(start, TILE)
            rows = rr[p, :, low:, tile].reshape(PLANE * (PAIR - low), TILE)
            total = contract(chosen, rows, 0, 0)
            par[pl.ds(p * 2 * FRAMES + begin, end - begin), tile] = total.astype(BF16)

    arrive(second[0])
    own[0].wait()
    own[1].wait()
    for c in range(2):
        for p in (2 * c, 2 * c + 1):
            arrive(rows_in[p, 0])
        forward(0, c)
        if c == 0:
            second.append(gather_second(1, first[1]))
    parts(0, 2)
    sums = [reduce_first(0)]
    parts(0, 1)
    parts(0, 3)
    reduce_alone(0)
    parts(0, 0)
    for c in range(2):
        backward(0, c)

    arrive(second[1])
    own[2].wait()
    own[3].wait()
    arrive(rows_in[0, 1] + rows_in[1, 1])
    forward(1, 0)
    backward(1, 0)
    sums[0] = reduce_second(0, sums[0])
    arrive(rows_in[2, 1])
    rows_back(3, 0)
    arrive(rows_in[3, 1])
    forward(1, 1)
    parts(1, 2)
    sums.append(reduce_first(1))
    backward(1, 1)
    rows_back(3, 1)
    for p in (2, 1, 0):
        pieces = [(EARLY, PAIR, columns) for columns in (HALVES if p == 0 else ((0, D),))]
        for low, high, columns in (*pieces, (0, EARLY, (0, D))):
            for m in range(LOCAL):
                rows_back(p, m, low, high, columns)
    parts(1, 1)
    parts(1, 3)
    reduce_alone(1)
    parts(1, 0)
    reduce_last(0, sums[0])

    def chunk(distance, half=None):
        start, size = SLOT[distance] * FRAMES, FRAMES
        if half is not None:
            size = FRAMES // 2
            start += half * size
        return pl.ds(start, size)

    def returned(p):
        arrive(back[p, 0, (0, D)])
        combine(p, 0, 0, 2 * FRAMES)

    def returned_second(p, columns=(0, D)):
        arrive(back[p, EARLY, columns])
        combine(p, EARLY, FRAMES, 2 * FRAMES, columns)

    def returned_first(p):
        arrive(back[p, 0, (0, D)])
        combine(p, 0, 0, FRAMES)

    def pass_on(way, distance, step, columns, to):
        part = pl.ds(*columns)
        add(par, (chunk(distance), part), zin[way, step, :, part])
        return send(par.at[chunk(distance), part], zin.at[way, step + 1, :, part], to)

    returned(3)
    up = send(par.at[chunk(4, 0)], zhalf.at[0], z_up)
    down = send(par.at[chunk(4, 1)], zhalf.at[1], z_down)
    returned_second(2)
    arrive([up])
    add(par, (chunk(3, 0),), zhalf[0])
    up = send(par.at[chunk(3)], zin.at[0, 0], z_up)
    arrive([down])
    add(par, (chunk(5, 1),), zhalf[1])
    down = send(par.at[chunk(5)], zin.at[1, 0], z_down)
    sums[1] = reduce_second(1, sums[1])
    returned_first(2)
    returned_second(1)
    arrive([up])
    up = [pass_on(0, 2, 0, columns, z_up) for columns in HALVES]
    arrive([down])
    down = [pass_on(1, 6, 0, columns, z_down) for columns in HALVES]
    returned_first(1)
    late = []
    for half, columns in enumerate(HALVES):
        arrive([down[half]])
        late.append(pass_on(1, 7, 1, columns, z_down_other))
        returned_second(0, columns)
        arrive([up[half]])
        late.append(pass_on(0, 1, 1, columns, z_up_other))
    returned_first(0)
    across = send(par.at[chunk(0)], fin, partner)
    reduce_last(1, sums[1])
    late.append(across)
    for copy in started:
        if all(copy is not other for other in late):
            copy.wait_send()
    arrive(late)
    total = fin[...].astype(F32) + zin[0, 2].astype(F32) + zin[1, 2].astype(F32)
    sent_ref[...] = total.astype(BF16)
    for copy in outputs:
        copy.wait()
    for copy in late:
        copy.wait_send()


def publish(sent_in, gi_in, go_in, sent_out, gi_out, go_out, sent_held, gi_held, go_held, sems):
    trios = []
    for m in range(LOCAL):
        trios.append((gi_in.at[m], gi_held.at[m], gi_out.at[m]))
        trios.append((go_in.at[m], go_held.at[m], go_out.at[m]))
    trios.append((sent_in, sent_held, sent_out))
    inward = [pltpu.make_async_copy(a, h, sems.at[0, i]) for i, (a, h, _) in enumerate(trios)]
    outward = [pltpu.make_async_copy(h, b, sems.at[1, i]) for i, (_, h, b) in enumerate(trios)]
    for copy in inward:
        copy.start()
    for arriving, leaving in zip(inward, outward):
        arriving.wait()
        leaving.start()
    for copy in outward:
        copy.wait()


def per_device(frames, cotangent, expert_ids, gate_weights, weight_in, weight_out):
    vmem = pl.BlockSpec(memory_space=pltpu.VMEM)
    anywhere = pl.BlockSpec(memory_space=pl.ANY)
    shapes = (
        jax.ShapeDtypeStruct((FRAMES, D), BF16),
        jax.ShapeDtypeStruct((LOCAL, QUARTER, H), BF16),
        jax.ShapeDtypeStruct((LOCAL, H, QUARTER), BF16),
    )
    results = pl.pallas_call(
        kernel,
        name="relay",
        out_shape=shapes,
        in_specs=[anywhere] * 6,
        out_specs=(vmem, anywhere, anywhere),
        scratch_shapes=[
            pltpu.VMEM((2, NZ * FRAMES, D), BF16),
            pltpu.VMEM((NZ, 16, FRAMES), F32),
            pltpu.VMEM((PAIRS, PLANE, PAIR, 2 * FRAMES), BF16),
            pltpu.VMEM((PAIRS, LOCAL, NX - 1, 2, PAIR, D), BF16),
            pltpu.VMEM((LOCAL, 2, ROWS, D), BF16),
            pltpu.VMEM((LOCAL, NY, QUARTER, H), BF16),
            pltpu.VMEM((LOCAL, NY, H, QUARTER), BF16),
            pltpu.VMEM((H, ROWS), BF16),
            pltpu.VMEM((ROWS, H), BF16),
            pltpu.VMEM((LOCAL, ROWS, D), BF16),
            pltpu.VMEM((PAIRS, PLANE, PAIR, D), BF16),
            pltpu.VMEM((NZ * FRAMES, D), BF16),
            pltpu.VMEM((2, FRAMES // 2, D), BF16),
            pltpu.VMEM((2, 3, FRAMES, D), BF16),
            pltpu.VMEM((LOCAL, NY, QUARTER, H), BF16),
            pltpu.VMEM((LOCAL, NY, H, QUARTER), BF16),
            pltpu.VMEM((LOCAL, 2, QUARTER // 2, H), BF16),
            pltpu.VMEM((LOCAL, 2, H // 2, QUARTER), BF16),
            pltpu.VMEM((LOCAL, 2, QUARTER, H), BF16),
            pltpu.VMEM((LOCAL, 2, H, QUARTER), BF16),
            pltpu.VMEM((FRAMES, D), BF16),
            pltpu.VMEM((8, FRAMES), jnp.int32),
            pltpu.SemaphoreType.DMA((COPIES,)),
            pltpu.SemaphoreType.DMA((COPIES,)),
            pltpu.SemaphoreType.DMA((LOCAL, 2)),
            pltpu.SemaphoreType.DMA((4 + 2 * LOCAL,)),
        ],
        compiler_params=pltpu.CompilerParams(
            collective_id=0, has_side_effects=True, vmem_limit_bytes=60 * 2**20
        ),
    )(expert_ids[0].T, gate_weights[0].T, frames[0], cotangent[0], weight_in[0], weight_out[0])
    sent, grad_in, grad_out = pl.pallas_call(
        publish,
        name="publish",
        out_shape=shapes,
        in_specs=[anywhere] * 3,
        out_specs=(anywhere,) * 3,
        scratch_shapes=[
            *[pltpu.VMEM(shape.shape, shape.dtype) for shape in shapes],
            pltpu.SemaphoreType.DMA((2, 1 + 2 * LOCAL)),
        ],
    )(*results)
    return sent[None], grad_in[None], grad_out[None]


def solution(mesh):
    rows = P("section", ("expert", "replica"), None)
    first = P("section", "expert", "replica", None)
    second = P("section", "expert", None, "replica")
    return jax.shard_map(
        per_device,
        mesh=mesh,
        in_specs=(rows, rows, rows, rows, first, second),
        out_specs=(rows, first, second),
        check_vma=False,
    )
```

```python
import jax
import jax.numpy as jnp
from jax import lax
from jax.experimental import pallas as pl
from jax.experimental.pallas import tpu as pltpu
from jax.sharding import PartitionSpec as P

MESH = pl.DeviceIdType.MESH
NZ, NX, NY = 8, 4, 4
FRAMES = 128
D, H = 1024, 768
MOST = 24
PAIR = 2 * MOST
LOCAL = 2
PLANE = NX * LOCAL
ROWS = NZ * NX * MOST
CHUNK = ROWS // 2
QUARTER = D // NY
TILE = 256
COPIES = 192
HALVES = ((0, D // 2), (D // 2, D // 2))
EARLY = 16
ORDER = (0, 1, 7, 2, 6, 3, 5, 4)
SLOT = {distance: place for place, distance in enumerate(ORDER)}
PAIRS = len(ORDER) // 2
F32, BF16 = jnp.float32, jnp.bfloat16


def contract(a, b, dim_a, dim_b):
    return lax.dot_general(a, b, (((dim_a,), (dim_b,)), ((), ())), preferred_element_type=F32)


def kernel(
    ids_ref,
    gate_ref,
    x_ref,
    c_ref,
    wi_ref,
    wo_ref,
    sent_ref,
    gi_ref,
    go_ref,
    tok,
    rt,
    hot,
    xs,
    xr,
    wi,
    wo,
    hb,
    pb,
    rg,
    rr,
    par,
    zhalf,
    zin,
    pi,
    po,
    hop_i,
    hop_o,
    end_i,
    end_o,
    fin,
    ids_held,
    send_sems,
    recv_sems,
    own_sems,
    local_sems,
):
    expert = lax.axis_index("expert")
    z, x = expert // NX, expert % NX
    y, s = lax.axis_index("replica"), lax.axis_index("section")

    def device(dz, dx, dy):
        place = lax.rem(z + dz + NZ, NZ) * NX + lax.rem(x + dx + NX, NX)
        return place, lax.rem(y + dy + NY, NY), s

    z_up, z_down = device(1, 0, 0), device(-1, 0, 0)
    y_up, y_down = device(0, 0, 1), device(0, 0, -1)
    x_far = [device(0, d, 0) for d in range(NX)]
    partner = (expert, y, 1 - s)

    z_up_other, z_down_other = (*z_up[:2], 1 - s), (*z_down[:2], 1 - s)
    barrier = pltpu.get_barrier_semaphore()
    peers = [z_up, z_down, y_up, y_down, *x_far[1:], partner, z_up_other, z_down_other]
    for peer in peers:
        pl.semaphore_signal(barrier, inc=1, device_id=peer, device_id_type=MESH)
    inputs = [
        pltpu.make_async_copy(src, dst, local_sems.at[i])
        for i, (src, dst) in enumerate(
            (
                (ids_ref, ids_held),
                (gate_ref, rt.at[0, pl.ds(8, 8)]),
                (x_ref, tok.at[0, pl.ds(0, FRAMES)]),
                (c_ref, tok.at[1, pl.ds(0, FRAMES)]),
            )
        )
    ]
    for copy in inputs:
        copy.start()

    started = []

    def send(src, dst, to):
        number = len(started)
        copy = pltpu.make_async_remote_copy(
            src_ref=src,
            dst_ref=dst,
            send_sem=send_sems.at[number],
            recv_sem=recv_sems.at[number],
            device_id=to,
            device_id_type=MESH,
        )
        copy.start()
        started.append(copy)
        return copy

    def arrive(copies):
        for copy in copies:
            copy.wait_recv()

    def hop_route(distance, step):
        to = z_up if step < 0 else z_down
        return [send(rt.at[SLOT[distance]], rt.at[SLOT[(distance + step) % NZ]], to)]

    def hop(distance, step, kind, half=None):
        land = (distance + step) % NZ
        to = z_up if step < 0 else z_down
        a, b, size = SLOT[distance] * FRAMES, SLOT[land] * FRAMES, FRAMES
        if half is not None:
            size = FRAMES // 2
            a, b = a + half * size, b + half * size
        return [send(tok.at[kind, pl.ds(a, size)], tok.at[kind, pl.ds(b, size)], to)]

    y_next, y_last = lax.rem(y + 1, NY), lax.rem(y + NY - 1, NY)

    def gather_first(m):
        return [
            send(ref.at[m], full.at[m, y], to)
            for to in (y_up, y_down)
            for ref, full in ((wi_ref, wi), (wo_ref, wo))
        ]

    def gather_second(m, first):
        arrive(first)
        copies = []
        for full, size in ((wi, QUARTER // 2), (wo, H // 2)):
            for place, half, to in ((y_last, 0, y_up), (y_next, 1, y_down)):
                part = full.at[m, place, pl.ds(half * size, size)]
                copies.append(send(part, part, to))
        return copies

    earlier = (
        lax.broadcasted_iota(jnp.int32, (FRAMES, FRAMES), 0)
        < lax.broadcasted_iota(jnp.int32, (FRAMES, FRAMES), 1)
    ).astype(BF16)
    place_row = lax.broadcasted_iota(jnp.int32, (PAIR, 2 * FRAMES), 0).astype(F32)
    members = [
        (z * PLANE + lax.rem(x + q // LOCAL, NX) * LOCAL + q % LOCAL).astype(F32)
        for q in range(PLANE)
    ]

    def routing(slot):
        ids, gates = rt[slot, pl.ds(0, 8), :], rt[slot, pl.ds(8, 8), :]
        gate = jnp.concatenate(
            [
                jnp.sum(jnp.where(ids == member, gates, 0.0), 0, keepdims=True)
                for member in members
            ],
            0,
        )
        named = jnp.where(gate > 0.0, 1.0, 0.0)
        place = jnp.dot(named.astype(BF16), earlier, preferred_element_type=F32)
        return gate, jnp.where(gate > 0.0, place, -100.0)

    inputs[0].wait()
    inputs[1].wait()
    rt[0, pl.ds(0, 8), :] = ids_held[...].astype(F32)
    own_gate, own_place = routing(0)
    own_match = [
        place_row[:EARLY, :FRAMES] == own_place[q : q + 1, :] for q in range(PLANE)
    ]
    own_hot = jnp.concatenate([jnp.where(match, 1.0, 0.0) for match in own_match], 0).astype(BF16)
    own_gate = jnp.concatenate(
        [
            jnp.sum(jnp.where(match, own_gate[q : q + 1, :], 0.0), 1, keepdims=True)
            for q, match in enumerate(own_match)
        ],
        0,
    )
    inputs[2].wait()
    inputs[3].wait()
    pl.semaphore_wait(barrier, len(peers))

    down_route, up_route = hop_route(0, 1), hop_route(0, -1)
    up, down = {}, {}
    for kind in range(2):
        down[kind] = hop(0, 1, kind)
        up[kind] = hop(0, -1, kind)
    first = [gather_first(0)]
    own = []
    for m in range(LOCAL):
        for k, (ref, full) in enumerate(((wi_ref, wi), (wo_ref, wo))):
            own.append(pltpu.make_async_copy(ref.at[m], full.at[m, y], own_sems.at[m, k]))
            own[-1].start()

    def prepare(p):
        gate_a, place_a = routing(2 * p)
        gate_b, place_b = routing(2 * p + 1)
        gate = jnp.concatenate([gate_a, gate_b], 1)
        place = jnp.concatenate([place_a, place_b + float(MOST)], 1)
        slot_gates = []
        for q in range(PLANE):
            match = place_row == place[q : q + 1, :]
            hot[p, q] = jnp.where(match, 1.0, 0.0).astype(BF16)
            slot_gates.append(
                jnp.sum(jnp.where(match, gate[q : q + 1, :], 0.0), 1, keepdims=True)
            )
        return jnp.concatenate(slot_gates, 0)

    def store(p, kind, rows, height, low, high, tile):
        for q in range(PLANE):
            d, m = q // LOCAL, q % LOCAL
            start = q * height + (low if height == PAIR else 0)
            block = rows[start : start + high - low]
            if d:
                xs[p, m, d - 1, kind, low:high, tile] = block
            else:
                xr[m, kind, pl.ds(p * NX * PAIR + low, high - low), tile] = block

    def pick(p, kind, slot_gate, low=0):
        source = pl.ds(p * 2 * FRAMES, 2 * FRAMES)
        chosen = hot[p].reshape(PLANE * PAIR, 2 * FRAMES)
        for start in range(0, D, TILE):
            tile = pl.ds(start, TILE)
            rows = jnp.dot(chosen, tok[kind, source, tile], preferred_element_type=F32)
            if kind:
                rows = rows * slot_gate
            store(p, kind, rows.astype(BF16), PAIR, low, PAIR, tile)

    rows_in = {(p, m): [] for p in range(PAIRS) for m in range(LOCAL)}

    def scatter(p, m, kind, low=0, high=PAIR):
        for d in range(1, NX):
            src = xs.at[p, m, d - 1, kind, pl.ds(low, high - low)]
            rows = pl.ds((p * NX + NX - d) * PAIR + low, high - low)
            rows_in[p, m].append(send(src, xr.at[m, kind, rows], x_far[d]))

    for kind in range(2):
        for start in range(0, D, TILE):
            tile = pl.ds(start, TILE)
            frames = tok[kind, pl.ds(0, FRAMES), tile]
            rows = jnp.dot(own_hot, frames, preferred_element_type=F32)
            if kind:
                rows = rows * own_gate
            store(0, kind, rows.astype(BF16), EARLY, 0, EARLY, tile)
        for m in range(LOCAL):
            scatter(0, m, kind, 0, EARLY)
    arrive(down_route)
    down_route = hop_route(1, 1)
    slot_gate = prepare(0)
    arrive(up_route)
    up_route = hop_route(7, -1)
    up_next, down_next = {}, {}
    for kind in range(2):
        arrive(down[kind])
        down_next[kind] = hop(1, 1, kind)
        arrive(up[kind])
        up_next[kind] = hop(7, -1, kind)
        pick(0, kind, slot_gate, EARLY)
        for m in range(LOCAL):
            scatter(0, m, kind, EARLY)
    up, down = up_next, down_next
    for p, (a, b) in ((1, (6, 2)), (2, (5, 3))):
        arrive(down_route)
        arrive(up_route)
        if p == 1:
            down_route = hop_route(b, 1)
        up_route = hop_route(a, -1)
        slot_gate = prepare(p)
        up_next, down_next = {}, {}
        for kind in range(2):
            arrive(down[kind])
            down_next[kind] = hop(b, 1, kind, 1 if p == 2 else None)
            arrive(up[kind])
            up_next[kind] = hop(a, -1, kind, 0 if p == 2 else None)
            pick(p, kind, slot_gate)
            scatter(p, 0, kind)
            if p == 1:
                scatter(p, 1, kind)
                if kind == 0:
                    second = [gather_second(0, first[0])]
                    first.append(gather_first(1))
        up, down = up_next, down_next
    arrive(up_route)
    slot_gate = prepare(3)
    for kind in range(2):
        arrive(down[kind] + up[kind])
        pick(3, kind, slot_gate)
        scatter(3, 0, kind)
    for p in (2, 3):
        for kind in range(2):
            scatter(p, 1, kind)

    def forward(m, c):
        rows = pl.ds(c * CHUNK, CHUNK)

        @pl.loop(0, H // TILE)
        def _(n):
            columns = pl.ds(pl.multiple_of(n * TILE, TILE), TILE)
            pre = jnp.zeros((CHUNK, TILE), F32)
            hidden_grad = jnp.zeros((CHUNK, TILE), F32)
            for r in range(NY):
                part = pl.ds(r * QUARTER, QUARTER)
                pre += contract(xr[m, 0, rows, part], wi[m, r, :, columns], 1, 0)
                hidden_grad += contract(xr[m, 1, rows, part], wo[m, r, columns, :], 1, 1)
            sigma = jax.nn.sigmoid(pre)
            slope = sigma * (1.0 + pre * (1.0 - sigma))
            hb[columns, rows] = jnp.transpose(pre * sigma).astype(BF16)
            pb[rows, columns] = (hidden_grad * slope).astype(BF16)

    def backward(m, c):
        rows = pl.ds(c * CHUNK, CHUNK)

        @pl.loop(0, NY)
        def _(r):
            columns = pl.ds(pl.multiple_of(r * QUARTER, QUARTER), QUARTER)
            rg[m, rows, columns] = contract(pb[rows, :], wi[m, r], 1, 1).astype(BF16)

    def parts(m, j):
        columns = pl.ds(pl.multiple_of(lax.rem(y + j, NY) * QUARTER, QUARTER), QUARTER)
        pi[m, j] = contract(xr[m, 0, :, columns], pb[...], 0, 0).astype(BF16)
        po[m, j] = contract(hb[...], xr[m, 1, :, columns], 1, 0).astype(BF16)

    half_i, half_o = QUARTER // 2, H // 2

    def reduce_first(m):
        copies = []
        for way, to in ((0, y_up), (1, y_down)):
            copies.append(send(pi.at[m, 2, pl.ds(way * half_i, half_i)], hop_i.at[m, way], to))
            copies.append(send(po.at[m, 2, pl.ds(way * half_o, half_o)], hop_o.at[m, way], to))
        return copies

    def add(ref, place, term):
        ref[place] = (ref[place].astype(F32) + term.astype(F32)).astype(BF16)

    ends = {(m, way): [] for m in range(LOCAL) for way in range(2)}

    def reduce_to(m, way, half, to):
        j = 1 if way == 0 else 3
        for part, end, size in ((pi, end_i, half_i), (po, end_o, half_o)):
            rows = pl.ds(half * size, size)
            ends[m, way].append(send(part.at[m, j, rows], end.at[m, way, rows], to))

    def reduce_alone(m):
        for way, to in ((0, y_up), (1, y_down)):
            reduce_to(m, way, 1 - way, to)

    def reduce_second(m, copies):
        for way, to in ((0, y_up), (1, y_down)):
            j = 1 if way == 0 else 3
            arrive(copies[2 * way : 2 * way + 2])
            add(pi, (m, j, pl.ds(way * half_i, half_i)), hop_i[m, way])
            add(po, (m, j, pl.ds(way * half_o, half_o)), hop_o[m, way])
            reduce_to(m, way, way, to)
        return ends[m, 0] + ends[m, 1]

    outputs = []

    def reduce_last(m, copies):
        arrive(copies)
        for k, (out, part, end) in enumerate(((gi_ref, pi, end_i), (go_ref, po, end_o))):
            total = part[m, 0].astype(F32) + end[m, 0].astype(F32) + end[m, 1].astype(F32)
            part[m, 0] = total.astype(BF16)
            outputs.append(
                pltpu.make_async_copy(part.at[m, 0], out.at[m], local_sems.at[4 + 2 * m + k])
            )
            outputs[-1].start()

    back = {}

    def rows_back(p, m, low=0, high=PAIR, columns=(0, D)):
        part = pl.ds(*columns)
        for b in range(1, NX):
            rows = pl.ds((p * NX + b) * PAIR + low, high - low)
            place = rr.at[p, (NX - b) * LOCAL + m, pl.ds(low, high - low), part]
            copy = send(rg.at[m, rows, part], place, x_far[b])
            back.setdefault((p, low, columns), []).append(copy)
        rr[p, m, low:high, part] = rg[m, pl.ds(p * NX * PAIR + low, high - low), part]

    def combine(p, low, begin, end, columns=(0, D)):
        chosen = hot[p, :, low:, begin:end].reshape(PLANE * (PAIR - low), end - begin)
        for start in range(columns[0], columns[0] + columns[1], TILE):
            tile = pl.ds(start, TILE)
            rows = rr[p, :, low:, tile].reshape(PLANE * (PAIR - low), TILE)
            total = contract(chosen, rows, 0, 0)
            par[pl.ds(p * 2 * FRAMES + begin, end - begin), tile] = total.astype(BF16)

    arrive(second[0])
    own[0].wait()
    own[1].wait()
    for c in range(2):
        for p in (2 * c, 2 * c + 1):
            arrive(rows_in[p, 0])
        forward(0, c)
        if c == 0:
            second.append(gather_second(1, first[1]))
    parts(0, 2)
    sums = [reduce_first(0)]
    parts(0, 1)
    parts(0, 3)
    reduce_alone(0)
    parts(0, 0)
    for c in range(2):
        backward(0, c)

    arrive(second[1])
    own[2].wait()
    own[3].wait()
    arrive(rows_in[0, 1] + rows_in[1, 1])
    forward(1, 0)
    backward(1, 0)
    sums[0] = reduce_second(0, sums[0])
    arrive(rows_in[2, 1])
    rows_back(3, 0)
    arrive(rows_in[3, 1])
    forward(1, 1)
    parts(1, 2)
    sums.append(reduce_first(1))
    backward(1, 1)
    rows_back(3, 1)
    for p in (2, 1, 0):
        pieces = [(EARLY, PAIR, columns) for columns in (HALVES if p == 0 else ((0, D),))]
        for low, high, columns in (*pieces, (0, EARLY, (0, D))):
            for m in range(LOCAL):
                rows_back(p, m, low, high, columns)
    parts(1, 1)
    parts(1, 3)
    reduce_alone(1)

    def chunk(distance, half=None):
        start, size = SLOT[distance] * FRAMES, FRAMES
        if half is not None:
            size = FRAMES // 2
            start += half * size
        return pl.ds(start, size)

    def returned(p):
        arrive(back[p, 0, (0, D)])
        combine(p, 0, 0, 2 * FRAMES)

    def returned_second(p, columns=(0, D)):
        arrive(back[p, EARLY, columns])
        combine(p, EARLY, FRAMES, 2 * FRAMES, columns)

    def returned_first(p):
        arrive(back[p, 0, (0, D)])
        combine(p, 0, 0, FRAMES)

    def pass_on(way, distance, step, columns, to):
        part = pl.ds(*columns)
        add(par, (chunk(distance), part), zin[way, step, :, part])
        return send(par.at[chunk(distance), part], zin.at[way, step + 1, :, part], to)

    returned(3)
    up = send(par.at[chunk(4, 0)], zhalf.at[0], z_up)
    down = send(par.at[chunk(4, 1)], zhalf.at[1], z_down)
    parts(1, 0)
    reduce_last(0, sums[0])
    returned_second(2)
    arrive([up])
    add(par, (chunk(3, 0),), zhalf[0])
    up = send(par.at[chunk(3)], zin.at[0, 0], z_up)
    arrive([down])
    add(par, (chunk(5, 1),), zhalf[1])
    down = send(par.at[chunk(5)], zin.at[1, 0], z_down)
    sums[1] = reduce_second(1, sums[1])
    returned_first(2)
    returned_second(1)
    arrive([up])
    up = [pass_on(0, 2, 0, columns, z_up) for columns in HALVES]
    arrive([down])
    down = [pass_on(1, 6, 0, columns, z_down) for columns in HALVES]
    returned_first(1)
    late = []
    for half, columns in enumerate(HALVES):
        arrive([down[half]])
        late.append(pass_on(1, 7, 1, columns, z_down_other))
        returned_second(0, columns)
        arrive([up[half]])
        late.append(pass_on(0, 1, 1, columns, z_up_other))
    returned_first(0)
    across = send(par.at[chunk(0)], fin, partner)
    reduce_last(1, sums[1])
    late.append(across)
    for copy in started:
        if all(copy is not other for other in late):
            copy.wait_send()
    arrive(late)
    total = fin[...].astype(F32) + zin[0, 2].astype(F32) + zin[1, 2].astype(F32)
    sent_ref[...] = total.astype(BF16)
    for copy in outputs:
        copy.wait()
    for copy in late:
        copy.wait_send()


def publish(sent_in, gi_in, go_in, sent_out, gi_out, go_out, sent_held, gi_held, go_held, sems):
    trios = []
    for m in range(LOCAL):
        trios.append((gi_in.at[m], gi_held.at[m], gi_out.at[m]))
        trios.append((go_in.at[m], go_held.at[m], go_out.at[m]))
    trios.append((sent_in, sent_held, sent_out))
    inward = [pltpu.make_async_copy(a, h, sems.at[0, i]) for i, (a, h, _) in enumerate(trios)]
    outward = [pltpu.make_async_copy(h, b, sems.at[1, i]) for i, (_, h, b) in enumerate(trios)]
    for copy in inward:
        copy.start()
    for arriving, leaving in zip(inward, outward):
        arriving.wait()
        leaving.start()
    for copy in outward:
        copy.wait()


def per_device(frames, cotangent, expert_ids, gate_weights, weight_in, weight_out):
    vmem = pl.BlockSpec(memory_space=pltpu.VMEM)
    anywhere = pl.BlockSpec(memory_space=pl.ANY)
    shapes = (
        jax.ShapeDtypeStruct((FRAMES, D), BF16),
        jax.ShapeDtypeStruct((LOCAL, QUARTER, H), BF16),
        jax.ShapeDtypeStruct((LOCAL, H, QUARTER), BF16),
    )
    results = pl.pallas_call(
        kernel,
        name="relay",
        out_shape=shapes,
        in_specs=[anywhere] * 6,
        out_specs=(vmem, anywhere, anywhere),
        scratch_shapes=[
            pltpu.VMEM((2, NZ * FRAMES, D), BF16),
            pltpu.VMEM((NZ, 16, FRAMES), F32),
            pltpu.VMEM((PAIRS, PLANE, PAIR, 2 * FRAMES), BF16),
            pltpu.VMEM((PAIRS, LOCAL, NX - 1, 2, PAIR, D), BF16),
            pltpu.VMEM((LOCAL, 2, ROWS, D), BF16),
            pltpu.VMEM((LOCAL, NY, QUARTER, H), BF16),
            pltpu.VMEM((LOCAL, NY, H, QUARTER), BF16),
            pltpu.VMEM((H, ROWS), BF16),
            pltpu.VMEM((ROWS, H), BF16),
            pltpu.VMEM((LOCAL, ROWS, D), BF16),
            pltpu.VMEM((PAIRS, PLANE, PAIR, D), BF16),
            pltpu.VMEM((NZ * FRAMES, D), BF16),
            pltpu.VMEM((2, FRAMES // 2, D), BF16),
            pltpu.VMEM((2, 3, FRAMES, D), BF16),
            pltpu.VMEM((LOCAL, NY, QUARTER, H), BF16),
            pltpu.VMEM((LOCAL, NY, H, QUARTER), BF16),
            pltpu.VMEM((LOCAL, 2, QUARTER // 2, H), BF16),
            pltpu.VMEM((LOCAL, 2, H // 2, QUARTER), BF16),
            pltpu.VMEM((LOCAL, 2, QUARTER, H), BF16),
            pltpu.VMEM((LOCAL, 2, H, QUARTER), BF16),
            pltpu.VMEM((FRAMES, D), BF16),
            pltpu.VMEM((8, FRAMES), jnp.int32),
            pltpu.SemaphoreType.DMA((COPIES,)),
            pltpu.SemaphoreType.DMA((COPIES,)),
            pltpu.SemaphoreType.DMA((LOCAL, 2)),
            pltpu.SemaphoreType.DMA((4 + 2 * LOCAL,)),
        ],
        compiler_params=pltpu.CompilerParams(
            collective_id=0, has_side_effects=True, vmem_limit_bytes=60 * 2**20
        ),
    )(expert_ids[0].T, gate_weights[0].T, frames[0], cotangent[0], weight_in[0], weight_out[0])
    sent, grad_in, grad_out = pl.pallas_call(
        publish,
        name="publish",
        out_shape=shapes,
        in_specs=[anywhere] * 3,
        out_specs=(anywhere,) * 3,
        scratch_shapes=[
            *[pltpu.VMEM(shape.shape, shape.dtype) for shape in shapes],
            pltpu.SemaphoreType.DMA((2, 1 + 2 * LOCAL)),
        ],
    )(*results)
    return sent[None], grad_in[None], grad_out[None]


def solution(mesh):
    rows = P("section", ("expert", "replica"), None)
    first = P("section", "expert", "replica", None)
    second = P("section", "expert", None, "replica")
    return jax.shard_map(
        per_device,
        mesh=mesh,
        in_specs=(rows, rows, rows, rows, first, second),
        out_specs=(rows, first, second),
        check_vma=False,
    )
```

```python
import jax
import jax.numpy as jnp
from jax import lax
from jax.experimental import pallas as pl
from jax.experimental.pallas import tpu as pltpu
from jax.sharding import PartitionSpec as P

MESH = pl.DeviceIdType.MESH
NZ, NX, NY = 8, 4, 4
FRAMES = 128
D, H = 1024, 768
MOST = 24
PAIR = 2 * MOST
LOCAL = 2
PLANE = NX * LOCAL
ROWS = NZ * NX * MOST
CHUNK = ROWS // 2
QUARTER = D // NY
TILE = 256
COPIES = 192
HALVES = ((0, D // 2), (D // 2, D // 2))
EARLY = 16
ORDER = (0, 1, 7, 2, 6, 3, 5, 4)
SLOT = {distance: place for place, distance in enumerate(ORDER)}
PAIRS = len(ORDER) // 2
F32, BF16 = jnp.float32, jnp.bfloat16


def contract(a, b, dim_a, dim_b):
    return lax.dot_general(a, b, (((dim_a,), (dim_b,)), ((), ())), preferred_element_type=F32)


def kernel(
    ids_ref,
    gate_ref,
    x_ref,
    c_ref,
    wi_ref,
    wo_ref,
    sent_ref,
    gi_ref,
    go_ref,
    tok,
    rt,
    hot,
    xs,
    xr,
    wi,
    wo,
    hb,
    pb,
    rg,
    rr,
    par,
    zhalf,
    zin,
    pi,
    po,
    hop_i,
    hop_o,
    end_i,
    end_o,
    fin,
    ids_held,
    send_sems,
    recv_sems,
    own_sems,
    local_sems,
):
    expert = lax.axis_index("expert")
    z, x = expert // NX, expert % NX
    y, s = lax.axis_index("replica"), lax.axis_index("section")

    def device(dz, dx, dy):
        place = lax.rem(z + dz + NZ, NZ) * NX + lax.rem(x + dx + NX, NX)
        return place, lax.rem(y + dy + NY, NY), s

    z_up, z_down = device(1, 0, 0), device(-1, 0, 0)
    y_up, y_down = device(0, 0, 1), device(0, 0, -1)
    x_far = [device(0, d, 0) for d in range(NX)]
    partner = (expert, y, 1 - s)

    z_up_other, z_down_other = (*z_up[:2], 1 - s), (*z_down[:2], 1 - s)
    barrier = pltpu.get_barrier_semaphore()
    peers = [z_up, z_down, y_up, y_down, *x_far[1:], partner, z_up_other, z_down_other]
    for peer in peers:
        pl.semaphore_signal(barrier, inc=1, device_id=peer, device_id_type=MESH)
    inputs = [
        pltpu.make_async_copy(src, dst, local_sems.at[i])
        for i, (src, dst) in enumerate(
            (
                (ids_ref, ids_held),
                (gate_ref, rt.at[0, pl.ds(8, 8)]),
                (x_ref, tok.at[0, pl.ds(0, FRAMES)]),
                (c_ref, tok.at[1, pl.ds(0, FRAMES)]),
            )
        )
    ]
    for copy in inputs:
        copy.start()

    started = []

    def send(src, dst, to):
        number = len(started)
        copy = pltpu.make_async_remote_copy(
            src_ref=src,
            dst_ref=dst,
            send_sem=send_sems.at[number],
            recv_sem=recv_sems.at[number],
            device_id=to,
            device_id_type=MESH,
        )
        copy.start()
        started.append(copy)
        return copy

    def arrive(copies):
        for copy in copies:
            copy.wait_recv()

    def hop_route(distance, step):
        to = z_up if step < 0 else z_down
        return [send(rt.at[SLOT[distance]], rt.at[SLOT[(distance + step) % NZ]], to)]

    def hop(distance, step, kind, half=None):
        land = (distance + step) % NZ
        to = z_up if step < 0 else z_down
        a, b, size = SLOT[distance] * FRAMES, SLOT[land] * FRAMES, FRAMES
        if half is not None:
            size = FRAMES // 2
            a, b = a + half * size, b + half * size
        return [send(tok.at[kind, pl.ds(a, size)], tok.at[kind, pl.ds(b, size)], to)]

    y_next, y_last = lax.rem(y + 1, NY), lax.rem(y + NY - 1, NY)

    def gather_first(m):
        return [
            send(ref.at[m], full.at[m, y], to)
            for to in (y_up, y_down)
            for ref, full in ((wi_ref, wi), (wo_ref, wo))
        ]

    def gather_second(m, first):
        arrive(first)
        copies = []
        for full, size in ((wi, QUARTER // 2), (wo, H // 2)):
            for place, half, to in ((y_last, 0, y_up), (y_next, 1, y_down)):
                part = full.at[m, place, pl.ds(half * size, size)]
                copies.append(send(part, part, to))
        return copies

    earlier = (
        lax.broadcasted_iota(jnp.int32, (FRAMES, FRAMES), 0)
        < lax.broadcasted_iota(jnp.int32, (FRAMES, FRAMES), 1)
    ).astype(BF16)
    place_row = lax.broadcasted_iota(jnp.int32, (PAIR, 2 * FRAMES), 0).astype(F32)
    members = [
        (z * PLANE + lax.rem(x + q // LOCAL, NX) * LOCAL + q % LOCAL).astype(F32)
        for q in range(PLANE)
    ]

    def routing(slot):
        ids, gates = rt[slot, pl.ds(0, 8), :], rt[slot, pl.ds(8, 8), :]
        gate = jnp.concatenate(
            [
                jnp.sum(jnp.where(ids == member, gates, 0.0), 0, keepdims=True)
                for member in members
            ],
            0,
        )
        named = jnp.where(gate > 0.0, 1.0, 0.0)
        place = jnp.dot(named.astype(BF16), earlier, preferred_element_type=F32)
        return gate, jnp.where(gate > 0.0, place, -100.0)

    inputs[0].wait()
    inputs[1].wait()
    rt[0, pl.ds(0, 8), :] = ids_held[...].astype(F32)
    own_gate, own_place = routing(0)
    own_match = [
        place_row[:EARLY, :FRAMES] == own_place[q : q + 1, :] for q in range(PLANE)
    ]
    own_hot = jnp.concatenate([jnp.where(match, 1.0, 0.0) for match in own_match], 0).astype(BF16)
    own_gate = jnp.concatenate(
        [
            jnp.sum(jnp.where(match, own_gate[q : q + 1, :], 0.0), 1, keepdims=True)
            for q, match in enumerate(own_match)
        ],
        0,
    )
    inputs[2].wait()
    inputs[3].wait()
    pl.semaphore_wait(barrier, len(peers))

    down_route, up_route = hop_route(0, 1), hop_route(0, -1)
    up, down = {}, {}
    for kind in range(2):
        down[kind] = hop(0, 1, kind)
        up[kind] = hop(0, -1, kind)
    first = [gather_first(0)]
    own = []
    for m in range(LOCAL):
        for k, (ref, full) in enumerate(((wi_ref, wi), (wo_ref, wo))):
            own.append(pltpu.make_async_copy(ref.at[m], full.at[m, y], own_sems.at[m, k]))
            own[-1].start()

    def prepare(p):
        gate_a, place_a = routing(2 * p)
        gate_b, place_b = routing(2 * p + 1)
        gate = jnp.concatenate([gate_a, gate_b], 1)
        place = jnp.concatenate([place_a, place_b + float(MOST)], 1)
        slot_gates = []
        for q in range(PLANE):
            match = place_row == place[q : q + 1, :]
            hot[p, q] = jnp.where(match, 1.0, 0.0).astype(BF16)
            slot_gates.append(
                jnp.sum(jnp.where(match, gate[q : q + 1, :], 0.0), 1, keepdims=True)
            )
        return jnp.concatenate(slot_gates, 0)

    def store(p, kind, rows, height, low, high, tile):
        for q in range(PLANE):
            d, m = q // LOCAL, q % LOCAL
            start = q * height + (low if height == PAIR else 0)
            block = rows[start : start + high - low]
            if d:
                xs[p, m, d - 1, kind, low:high, tile] = block
            else:
                xr[m, kind, pl.ds(p * NX * PAIR + low, high - low), tile] = block

    def pick(p, kind, slot_gate, low=0):
        source = pl.ds(p * 2 * FRAMES, 2 * FRAMES)
        chosen = hot[p].reshape(PLANE * PAIR, 2 * FRAMES)
        for start in range(0, D, TILE):
            tile = pl.ds(start, TILE)
            rows = jnp.dot(chosen, tok[kind, source, tile], preferred_element_type=F32)
            if kind:
                rows = rows * slot_gate
            store(p, kind, rows.astype(BF16), PAIR, low, PAIR, tile)

    rows_in = {(p, m): [] for p in range(PAIRS) for m in range(LOCAL)}

    def scatter(p, m, kind, low=0, high=PAIR):
        for d in range(1, NX):
            src = xs.at[p, m, d - 1, kind, pl.ds(low, high - low)]
            rows = pl.ds((p * NX + NX - d) * PAIR + low, high - low)
            rows_in[p, m].append(send(src, xr.at[m, kind, rows], x_far[d]))

    for kind in range(2):
        for start in range(0, D, TILE):
            tile = pl.ds(start, TILE)
            frames = tok[kind, pl.ds(0, FRAMES), tile]
            rows = jnp.dot(own_hot, frames, preferred_element_type=F32)
            if kind:
                rows = rows * own_gate
            store(0, kind, rows.astype(BF16), EARLY, 0, EARLY, tile)
        for m in range(LOCAL):
            scatter(0, m, kind, 0, EARLY)
    arrive(down_route)
    down_route = hop_route(1, 1)
    slot_gate = prepare(0)
    arrive(up_route)
    up_route = hop_route(7, -1)
    up_next, down_next = {}, {}
    for kind in range(2):
        arrive(down[kind])
        down_next[kind] = hop(1, 1, kind)
        arrive(up[kind])
        up_next[kind] = hop(7, -1, kind)
        pick(0, kind, slot_gate, EARLY)
        for m in range(LOCAL):
            scatter(0, m, kind, EARLY)
    up, down = up_next, down_next
    for p, (a, b) in ((1, (6, 2)), (2, (5, 3))):
        arrive(down_route)
        arrive(up_route)
        if p == 1:
            down_route = hop_route(b, 1)
        up_route = hop_route(a, -1)
        slot_gate = prepare(p)
        up_next, down_next = {}, {}
        for kind in range(2):
            arrive(down[kind])
            down_next[kind] = hop(b, 1, kind, 1 if p == 2 else None)
            arrive(up[kind])
            up_next[kind] = hop(a, -1, kind, 0 if p == 2 else None)
            pick(p, kind, slot_gate)
            scatter(p, 0, kind)
            if p == 1:
                scatter(p, 1, kind)
                if kind == 0:
                    second = [gather_second(0, first[0])]
                    first.append(gather_first(1))
        up, down = up_next, down_next
    arrive(up_route)
    slot_gate = prepare(3)
    for kind in range(2):
        arrive(down[kind] + up[kind])
        pick(3, kind, slot_gate)
        scatter(3, 0, kind)
    for p in (2, 3):
        for kind in range(2):
            scatter(p, 1, kind)

    def forward(m, c):
        rows = pl.ds(c * CHUNK, CHUNK)

        @pl.loop(0, H // TILE)
        def _(n):
            columns = pl.ds(pl.multiple_of(n * TILE, TILE), TILE)
            pre = jnp.zeros((CHUNK, TILE), F32)
            hidden_grad = jnp.zeros((CHUNK, TILE), F32)
            for r in range(NY):
                part = pl.ds(r * QUARTER, QUARTER)
                pre += contract(xr[m, 0, rows, part], wi[m, r, :, columns], 1, 0)
                hidden_grad += contract(xr[m, 1, rows, part], wo[m, r, columns, :], 1, 1)
            sigma = jax.nn.sigmoid(pre)
            slope = sigma * (1.0 + pre * (1.0 - sigma))
            hb[columns, rows] = jnp.transpose(pre * sigma).astype(BF16)
            pb[rows, columns] = (hidden_grad * slope).astype(BF16)

    def backward(m, c):
        rows = pl.ds(c * CHUNK, CHUNK)

        @pl.loop(0, NY)
        def _(r):
            columns = pl.ds(pl.multiple_of(r * QUARTER, QUARTER), QUARTER)
            rg[m, rows, columns] = contract(pb[rows, :], wi[m, r], 1, 1).astype(BF16)

    def parts(m, j):
        columns = pl.ds(pl.multiple_of(lax.rem(y + j, NY) * QUARTER, QUARTER), QUARTER)
        pi[m, j] = contract(xr[m, 0, :, columns], pb[...], 0, 0).astype(BF16)
        po[m, j] = contract(hb[...], xr[m, 1, :, columns], 1, 0).astype(BF16)

    half_i, half_o = QUARTER // 2, H // 2

    def reduce_first(m):
        copies = []
        for way, to in ((0, y_up), (1, y_down)):
            copies.append(send(pi.at[m, 2, pl.ds(way * half_i, half_i)], hop_i.at[m, way], to))
            copies.append(send(po.at[m, 2, pl.ds(way * half_o, half_o)], hop_o.at[m, way], to))
        return copies

    def add(ref, place, term):
        ref[place] = (ref[place].astype(F32) + term.astype(F32)).astype(BF16)

    ends = {(m, way): [] for m in range(LOCAL) for way in range(2)}

    def reduce_to(m, way, half, to):
        j = 1 if way == 0 else 3
        for part, end, size in ((pi, end_i, half_i), (po, end_o, half_o)):
            rows = pl.ds(half * size, size)
            ends[m, way].append(send(part.at[m, j, rows], end.at[m, way, rows], to))

    def reduce_alone(m):
        for way, to in ((0, y_up), (1, y_down)):
            reduce_to(m, way, 1 - way, to)

    def reduce_second(m, copies):
        for way, to in ((0, y_up), (1, y_down)):
            j = 1 if way == 0 else 3
            arrive(copies[2 * way : 2 * way + 2])
            add(pi, (m, j, pl.ds(way * half_i, half_i)), hop_i[m, way])
            add(po, (m, j, pl.ds(way * half_o, half_o)), hop_o[m, way])
            reduce_to(m, way, way, to)
        return ends[m, 0] + ends[m, 1]

    outputs = []

    def reduce_last(m, copies):
        arrive(copies)
        for k, (out, part, end) in enumerate(((gi_ref, pi, end_i), (go_ref, po, end_o))):
            total = part[m, 0].astype(F32) + end[m, 0].astype(F32) + end[m, 1].astype(F32)
            part[m, 0] = total.astype(BF16)
            outputs.append(
                pltpu.make_async_copy(part.at[m, 0], out.at[m], local_sems.at[4 + 2 * m + k])
            )
            outputs[-1].start()

    back = {}

    def rows_back(p, m, low=0, high=PAIR, columns=(0, D)):
        part = pl.ds(*columns)
        for b in range(1, NX):
            rows = pl.ds((p * NX + b) * PAIR + low, high - low)
            place = rr.at[p, (NX - b) * LOCAL + m, pl.ds(low, high - low), part]
            copy = send(rg.at[m, rows, part], place, x_far[b])
            back.setdefault((p, low, columns), []).append(copy)
        rr[p, m, low:high, part] = rg[m, pl.ds(p * NX * PAIR + low, high - low), part]

    def combine(p, low, begin, end, columns=(0, D)):
        chosen = hot[p, :, low:, begin:end].reshape(PLANE * (PAIR - low), end - begin)
        for start in range(columns[0], columns[0] + columns[1], TILE):
            tile = pl.ds(start, TILE)
            rows = rr[p, :, low:, tile].reshape(PLANE * (PAIR - low), TILE)
            total = contract(chosen, rows, 0, 0)
            par[pl.ds(p * 2 * FRAMES + begin, end - begin), tile] = total.astype(BF16)

    arrive(second[0])
    own[0].wait()
    own[1].wait()
    for c in range(2):
        for p in (2 * c, 2 * c + 1):
            arrive(rows_in[p, 0])
        forward(0, c)
        if c == 0:
            second.append(gather_second(1, first[1]))
    parts(0, 2)
    sums = [reduce_first(0)]
    parts(0, 1)
    parts(0, 3)
    reduce_alone(0)
    parts(0, 0)
    for c in range(2):
        backward(0, c)

    arrive(second[1])
    own[2].wait()
    own[3].wait()
    arrive(rows_in[0, 1] + rows_in[1, 1])
    forward(1, 0)
    backward(1, 0)
    sums[0] = reduce_second(0, sums[0])
    arrive(rows_in[2, 1])
    rows_back(3, 0)
    arrive(rows_in[3, 1])
    forward(1, 1)
    backward(1, 1)
    rows_back(3, 1)
    parts(1, 2)
    sums.append(reduce_first(1))
    for p in (2, 1, 0):
        pieces = [(EARLY, PAIR, columns) for columns in (HALVES if p == 0 else ((0, D),))]
        for low, high, columns in (*pieces, (0, EARLY, (0, D))):
            for m in range(LOCAL):
                rows_back(p, m, low, high, columns)
    parts(1, 1)
    parts(1, 3)
    reduce_alone(1)

    def chunk(distance, half=None):
        start, size = SLOT[distance] * FRAMES, FRAMES
        if half is not None:
            size = FRAMES // 2
            start += half * size
        return pl.ds(start, size)

    def returned(p):
        arrive(back[p, 0, (0, D)])
        combine(p, 0, 0, 2 * FRAMES)

    def returned_second(p, columns=(0, D)):
        arrive(back[p, EARLY, columns])
        combine(p, EARLY, FRAMES, 2 * FRAMES, columns)

    def returned_first(p):
        arrive(back[p, 0, (0, D)])
        combine(p, 0, 0, FRAMES)

    def pass_on(way, distance, step, columns, to):
        part = pl.ds(*columns)
        add(par, (chunk(distance), part), zin[way, step, :, part])
        return send(par.at[chunk(distance), part], zin.at[way, step + 1, :, part], to)

    returned(3)
    up = send(par.at[chunk(4, 0)], zhalf.at[0], z_up)
    down = send(par.at[chunk(4, 1)], zhalf.at[1], z_down)
    parts(1, 0)
    reduce_last(0, sums[0])
    returned_second(2)
    arrive([up])
    add(par, (chunk(3, 0),), zhalf[0])
    up = send(par.at[chunk(3)], zin.at[0, 0], z_up)
    arrive([down])
    add(par, (chunk(5, 1),), zhalf[1])
    down = send(par.at[chunk(5)], zin.at[1, 0], z_down)
    sums[1] = reduce_second(1, sums[1])
    returned_first(2)
    returned_second(1)
    arrive([up])
    up = [pass_on(0, 2, 0, columns, z_up) for columns in HALVES]
    arrive([down])
    down = [pass_on(1, 6, 0, columns, z_down) for columns in HALVES]
    returned_first(1)
    late = []
    for half, columns in enumerate(HALVES):
        arrive([down[half]])
        late.append(pass_on(1, 7, 1, columns, z_down_other))
        returned_second(0, columns)
        arrive([up[half]])
        late.append(pass_on(0, 1, 1, columns, z_up_other))
    returned_first(0)
    across = send(par.at[chunk(0)], fin, partner)
    reduce_last(1, sums[1])
    late.append(across)
    for copy in started:
        if all(copy is not other for other in late):
            copy.wait_send()
    arrive(late)
    total = fin[...].astype(F32) + zin[0, 2].astype(F32) + zin[1, 2].astype(F32)
    sent_ref[...] = total.astype(BF16)
    for copy in outputs:
        copy.wait()
    for copy in late:
        copy.wait_send()


def publish(sent_in, gi_in, go_in, sent_out, gi_out, go_out, sent_held, gi_held, go_held, sems):
    trios = []
    for m in range(LOCAL):
        trios.append((gi_in.at[m], gi_held.at[m], gi_out.at[m]))
        trios.append((go_in.at[m], go_held.at[m], go_out.at[m]))
    trios.append((sent_in, sent_held, sent_out))
    inward = [pltpu.make_async_copy(a, h, sems.at[0, i]) for i, (a, h, _) in enumerate(trios)]
    outward = [pltpu.make_async_copy(h, b, sems.at[1, i]) for i, (_, h, b) in enumerate(trios)]
    for copy in inward:
        copy.start()
    for arriving, leaving in zip(inward, outward):
        arriving.wait()
        leaving.start()
    for copy in outward:
        copy.wait()


def per_device(frames, cotangent, expert_ids, gate_weights, weight_in, weight_out):
    vmem = pl.BlockSpec(memory_space=pltpu.VMEM)
    anywhere = pl.BlockSpec(memory_space=pl.ANY)
    shapes = (
        jax.ShapeDtypeStruct((FRAMES, D), BF16),
        jax.ShapeDtypeStruct((LOCAL, QUARTER, H), BF16),
        jax.ShapeDtypeStruct((LOCAL, H, QUARTER), BF16),
    )
    results = pl.pallas_call(
        kernel,
        name="relay",
        out_shape=shapes,
        in_specs=[anywhere] * 6,
        out_specs=(vmem, anywhere, anywhere),
        scratch_shapes=[
            pltpu.VMEM((2, NZ * FRAMES, D), BF16),
            pltpu.VMEM((NZ, 16, FRAMES), F32),
            pltpu.VMEM((PAIRS, PLANE, PAIR, 2 * FRAMES), BF16),
            pltpu.VMEM((PAIRS, LOCAL, NX - 1, 2, PAIR, D), BF16),
            pltpu.VMEM((LOCAL, 2, ROWS, D), BF16),
            pltpu.VMEM((LOCAL, NY, QUARTER, H), BF16),
            pltpu.VMEM((LOCAL, NY, H, QUARTER), BF16),
            pltpu.VMEM((H, ROWS), BF16),
            pltpu.VMEM((ROWS, H), BF16),
            pltpu.VMEM((LOCAL, ROWS, D), BF16),
            pltpu.VMEM((PAIRS, PLANE, PAIR, D), BF16),
            pltpu.VMEM((NZ * FRAMES, D), BF16),
            pltpu.VMEM((2, FRAMES // 2, D), BF16),
            pltpu.VMEM((2, 3, FRAMES, D), BF16),
            pltpu.VMEM((LOCAL, NY, QUARTER, H), BF16),
            pltpu.VMEM((LOCAL, NY, H, QUARTER), BF16),
            pltpu.VMEM((LOCAL, 2, QUARTER // 2, H), BF16),
            pltpu.VMEM((LOCAL, 2, H // 2, QUARTER), BF16),
            pltpu.VMEM((LOCAL, 2, QUARTER, H), BF16),
            pltpu.VMEM((LOCAL, 2, H, QUARTER), BF16),
            pltpu.VMEM((FRAMES, D), BF16),
            pltpu.VMEM((8, FRAMES), jnp.int32),
            pltpu.SemaphoreType.DMA((COPIES,)),
            pltpu.SemaphoreType.DMA((COPIES,)),
            pltpu.SemaphoreType.DMA((LOCAL, 2)),
            pltpu.SemaphoreType.DMA((4 + 2 * LOCAL,)),
        ],
        compiler_params=pltpu.CompilerParams(
            collective_id=0, has_side_effects=True, vmem_limit_bytes=60 * 2**20
        ),
    )(expert_ids[0].T, gate_weights[0].T, frames[0], cotangent[0], weight_in[0], weight_out[0])
    sent, grad_in, grad_out = pl.pallas_call(
        publish,
        name="publish",
        out_shape=shapes,
        in_specs=[anywhere] * 3,
        out_specs=(anywhere,) * 3,
        scratch_shapes=[
            *[pltpu.VMEM(shape.shape, shape.dtype) for shape in shapes],
            pltpu.SemaphoreType.DMA((2, 1 + 2 * LOCAL)),
        ],
    )(*results)
    return sent[None], grad_in[None], grad_out[None]


def solution(mesh):
    rows = P("section", ("expert", "replica"), None)
    first = P("section", "expert", "replica", None)
    second = P("section", "expert", None, "replica")
    return jax.shard_map(
        per_device,
        mesh=mesh,
        in_specs=(rows, rows, rows, rows, first, second),
        out_specs=(rows, first, second),
        check_vma=False,
    )
```
